128 devices in a mesh: dp: 4 (over y_lo, core), code: 32 (over x, y_hi, z).
Axes of the slice: x: 4, y: 4 (y_hi: 2, y_lo: 2; y = y_hi * 2 + y_lo), z: 4, core: 2. Of those that a mesh axis runs over, the one named last changes fastest.
Arguments:
- latents: bfloat16 [2, 1024, 256], P(None, 'dp'), may hold values from -4 to 4
- cotangent: bfloat16 [2, 1024, 256], P(None, 'dp'), may hold values from -6 to 6
- saved_lse: float32 [2, 1024], P(None, 'dp'), as said below
- codebook: float32 [262144, 256], P(('dp', 'code')), may hold values from -4 to 4
- first_moment: float32 [262144, 256], P(('dp', 'code')), may hold values from -0.6 to 0.6
- second_moment: float32 [262144, 256], P(('dp', 'code')), may hold values from 0.001 to 0.1
Outputs:
- latent_grads: bfloat16 [2, 1024, 256], P(None, 'dp')
- new_codebook: float32 [262144, 256], P(('dp', 'code'))
- new_first: float32 [262144, 256], P(('dp', 'code'))
- new_second: float32 [262144, 256], P(('dp', 'code'))
The draws below stay inside these ranges and needn't reach their ends.
Inputs may be any that keep to these rules, and one draw needn't show every extreme that they name: `saved_lse`: for each row, the log of the sum over all 262144 codes of exp of the logits of the weights step, from these latents and this codebook.
All inputs are finite; a program needn't handle non-finite values.
Results may differ from the reference program's by a relative error of at most 0.035.
Values may be sent and summed in bfloat16 or wider, within the bound.
A program may use at most 128 MiB of HBM per device.

```python
import math
import jax
import jax.numpy as jnp
from jax import lax

WIDTH = 256
CODE_DEV = 2048
MICRO_BATCHES = 2
ADAM_STEPS = 10
CODES = 262144
BATCH = 1024


draw_sharpness = 0.25


def mixed_values(keys, shape):
    normal_part = jax.random.normal(keys[0], shape, jnp.float32)
    return normal_part


def shared_arrays(key):
    keys = jax.random.split(key, 12)
    code_scale = math.sqrt(48.0 / WIDTH)
    block_count = CODES // CODE_DEV
    centres = jax.random.normal(keys[9], (block_count, 1, WIDTH), jnp.float32) * math.sqrt(16.0 / WIDTH)
    factors = jnp.exp(jax.random.uniform(keys[10], (block_count, 1, 1), jnp.float32, -0.2, 0.2))
    spread_part = mixed_values(keys[0:3], (block_count, CODE_DEV, WIDTH)) * math.sqrt(32.0 / WIDTH)
    codebook = jnp.clip((factors * (centres + spread_part)).reshape(CODES, WIDTH), -4.0, 4.0)
    first_index = jax.random.randint(keys[3], (MICRO_BATCHES, BATCH), 0, CODES)
    second_index = jax.random.randint(keys[11], (MICRO_BATCHES, BATCH), 0, CODES)
    first_rows = codebook[first_index]
    second_rows = codebook[second_index]
    mixture = jax.random.uniform(keys[4], (MICRO_BATCHES, BATCH, 1), jnp.float32, 0.47, 0.53)
    noise = mixed_values(keys[5:8], (MICRO_BATCHES, BATCH, WIDTH))
    centre = 2.0 * (mixture * first_rows + (1.0 - mixture) * second_rows)
    latents = centre + 0.1 * code_scale * noise
    latents = jnp.clip(latents, -4.0, 4.0)
    return (latents.astype(jnp.bfloat16), codebook)


def log_totals(latents, codebook):
    flat_rows = latents.reshape(MICRO_BATCHES * BATCH, WIDTH)
    blocks = codebook.astype(jnp.bfloat16).reshape(CODES // CODE_DEV, CODE_DEV, WIDTH)

    def advance(carry, block):
        highest, total = carry
        squares = jnp.sum(jnp.square(block.astype(jnp.float32)), axis=1)
        logits = draw_sharpness * jnp.dot(flat_rows, block.T, preferred_element_type=jnp.float32) - 0.5 * draw_sharpness * squares[None, :]
        new_high = jnp.maximum(highest, jnp.max(logits, axis=1))
        total = total * jnp.exp(highest - new_high) + jnp.sum(jnp.exp(logits - new_high[:, None]), axis=1)
        return ((new_high, total), None)
    start = (jnp.full((MICRO_BATCHES * BATCH,), -1e+30, jnp.float32), jnp.zeros((MICRO_BATCHES * BATCH,), jnp.float32))
    (highest, total), _ = lax.scan(advance, start, blocks)
    return (highest + jnp.log(total)).reshape(MICRO_BATCHES, BATCH)


def draw_latents(key, part):
    latents, codebook = shared_arrays(key)
    return latents


def draw_codebook(key, part):
    latents, codebook = shared_arrays(key)
    return codebook


def draw_saved_lse(key, part):
    latents, codebook = shared_arrays(key)
    return log_totals(latents, codebook)


def block_scale(key, dims, cuts, least, top_value):
    gain, own = 1.0, jax.random.fold_in(key, 6)
    for dim, shards_of in cuts:
        draws = jnp.exp(jax.random.uniform(jax.random.fold_in(own, dim), (shards_of,), jnp.float32, least / len(cuts), top_value / len(cuts)))
        gain = gain * jnp.repeat(draws, dims[dim] // shards_of).reshape([-1 if axis == dim else 1 for axis in range(len(dims))])
    return gain


def normal_values(stream_key, dims, scale, bound, cuts=(), held_as=jnp.bfloat16):
    factor_of = block_scale(stream_key, dims, cuts, -0.22, 0.18) if cuts else 1.0
    array = jax.random.normal(stream_key, dims, jnp.float32) * scale * factor_of
    return jnp.minimum(jnp.maximum(array, -bound), bound).astype(held_as)


def setup_inputs(seed: int = 0) -> dict:
    seeds = jax.random.split(jax.random.key(seed), 7)
    latents = draw_latents(jax.random.fold_in(seeds[6], 71), 0)
    cotangent = normal_values(seeds[1], (MICRO_BATCHES, BATCH, WIDTH), 1.0, 6.0, ((1, 4),))
    saved_lse = draw_saved_lse(jax.random.fold_in(seeds[6], 71), 0)
    codebook = draw_codebook(jax.random.fold_in(seeds[6], 71), 0)
    first_moment = normal_values(seeds[4], (CODES, WIDTH), 0.1, 0.6, ((0, 128),), jnp.float32)
    second_moment = jnp.clip(jnp.exp(math.log(0.1) - 4.6051702 * jax.random.uniform(seeds[5], (CODES, WIDTH), jnp.float32) ** block_scale(seeds[5], (CODES, WIDTH), ((0, 128),), -0.2, 0.2)), 0.001, 0.1)
    return {"latents": latents, "cotangent": cotangent, "saved_lse": saved_lse, "codebook": codebook, "first_moment": first_moment, "second_moment": second_moment}


sharpness = 0.25
first_decay = 0.5
second_decay = 0.9
step_rate = 0.01
epsilon = 1e-08

def block_weights(rows_lat, rows_cot, saved, block):
    squares = lax.optimization_barrier(jnp.sum(jnp.square(block.astype(jnp.float32)), axis=1))
    logits = sharpness * jnp.dot(rows_lat, block.T, preferred_element_type=jnp.float32) - 0.5 * sharpness * squares[None, :]
    weights = jnp.exp(logits - saved[:, None])
    inner_dots = jnp.dot(rows_cot, block.T, preferred_element_type=jnp.float32)
    return (weights, inner_dots)

def micro_batch(rows_lat, rows_cot, saved, blocks):

    def first_pass(total, block):
        weights, inner_dots = block_weights(rows_lat, rows_cot, saved, block)
        return (total + lax.optimization_barrier(jnp.sum(weights * inner_dots, axis=1)), None)
    row_ratio, _ = lax.scan(first_pass, jnp.zeros((rows_lat.shape[0],), jnp.float32), blocks)

    def second_pass(total, block):
        weights, inner_dots = block_weights(rows_lat, rows_cot, saved, block)
        scaled = sharpness * weights * (inner_dots - row_ratio[:, None])
        scaled_half = scaled.astype(jnp.bfloat16)
        weights_half = weights.astype(jnp.bfloat16)
        total = total + jnp.dot(scaled_half, block, preferred_element_type=jnp.float32)
        grads = jnp.dot(weights_half.T, rows_cot, preferred_element_type=jnp.float32)
        grads = grads + jnp.dot(scaled_half.T, rows_lat, preferred_element_type=jnp.float32)
        grads = grads - lax.optimization_barrier(jnp.sum(scaled, axis=0))[:, None] * block.astype(jnp.float32)
        return (total, grads)
    start = jnp.zeros((rows_lat.shape[0], WIDTH), jnp.float32)
    latent_grad, code_grads = lax.scan(second_pass, start, blocks)
    return (latent_grad.astype(jnp.bfloat16), code_grads.reshape(CODES, WIDTH))

def reference(latents, cotangent, saved_lse, codebook, first_moment, second_moment):
    table = codebook.astype(jnp.bfloat16)
    blocks = table.reshape(CODES // CODE_DEV, CODE_DEV, WIDTH)
    results = []
    grad = jnp.zeros((CODES, WIDTH), jnp.float32)
    for batch_index in range(MICRO_BATCHES):
        latent_grad, code_grad = micro_batch(latents[batch_index], cotangent[batch_index], saved_lse[batch_index], blocks)
        results.append(latent_grad)
        grad = grad + code_grad
    new_first = first_decay * first_moment + (1.0 - first_decay) * grad
    new_second = second_decay * second_moment + (1.0 - second_decay) * grad * grad
    first_hat = new_first / (1.0 - first_decay ** ADAM_STEPS)
    second_hat = new_second / (1.0 - second_decay ** ADAM_STEPS)
    new_codebook = codebook - step_rate * first_hat / (jnp.sqrt(second_hat) + epsilon)
    return (jnp.stack(results, axis=0), new_codebook, new_first, new_second)
```

```python
import functools
import math

import jax
import jax.numpy as jnp
from jax import lax
from jax.experimental import pallas as pl
from jax.experimental.pallas import tpu as pltpu
from jax.sharding import PartitionSpec as P

MESH = pl.DeviceIdType.MESH
ADAM_STEPS = 10
sharpness = 0.25
first_decay = 0.5
second_decay = 0.9
step_rate = 0.01
epsilon = 1e-8

LOG2E = math.log2(math.e)
CODES = 2048
WIDTH = 256
ROWS = 256
BATCH = 1024
ALL = 2 * BATCH
F32, BF16 = jnp.float32, jnp.bfloat16


def place():
    dp, code = lax.axis_index("dp"), lax.axis_index("code")
    return code // 8, ((code // 4) % 2) * 2 + dp // 2, code % 4, dp % 2


def device(x, y, z, core):
    x, y, z, core = x % 4, y % 4, z % 4, core % 2
    return ((y % 2) * 2 + core, x * 8 + (y // 2) * 4 + z)


def dot_nt(a, b):
    return lax.dot_general(a, b, (((1,), (1,)), ((), ())), preferred_element_type=F32)


def dot(a, b):
    return jnp.dot(a, b, preferred_element_type=F32)


def aligned(v, n):
    return pl.multiple_of(v, n)


def kernel(
    lat_in, cot_in, lse_in, code_in, first_in, second_in,
    lg_out, code_out, first_out, second_out,
    lat, cot, lse, book, mom1, mom2, tab, tab_t, tab4, bias, weights, dots, scaled, grads, col_sum,
    part, part_y, part_s, part_xz, ratio,
    lg_part, lg_core, lg_pair, lg_y, lg_half, lg_xz, lg_final, lg_all,
    load_sem, gs_sem, gr_sem, fs_sem, fr_sem, cs_sem, cr_sem,
    ays_sem, ayr_sem, axs_sem, axr_sem,
    lcs_sem, lcr_sem, lys_sem, lyr_sem, lxs_sem, lxr_sem, lgs_sem, lgr_sem,
):
    x, y, z, core = place()
    y_lo, y_hi = y % 2, y // 2
    dp = y_lo * 2 + core
    part_no = x * 4 + z
    partner = device(x, y, z, core + 1)

    barrier = pltpu.get_barrier_semaphore()

    def yc_peer(i):
        return device(x, y + i // 2, z, core + i)

    def xz_peer(i):
        return device(x + i // 4, y, z + i, core)

    def code_peer(i):
        return device(x + i // 4, y + (i // 16) * 2, z + i, core)

    def signal_yc(i, _):
        pl.semaphore_signal(barrier, inc=1, device_id=yc_peer(i), device_id_type=MESH)
        return 0

    def signal_code(i, _):
        pl.semaphore_signal(barrier, inc=1, device_id=code_peer(i), device_id_type=MESH)
        return 0

    lax.fori_loop(1, 8, signal_yc, 0)
    lax.fori_loop(1, 32, signal_code, 0)

    book_copy = pltpu.make_async_copy(code_in, book, load_sem.at[0])
    book_copy.start()
    mom1_copy = pltpu.make_async_copy(first_in, mom1, load_sem.at[1])
    mom2_copy = pltpu.make_async_copy(second_in, mom2, load_sem.at[2])

    def rows_of(mb, owner):
        return pl.ds(aligned(mb * BATCH + owner * ROWS, ROWS), ROWS)

    own_copies = []
    for mb in range(2):
        own_copies += [
            pltpu.make_async_copy(lat_in.at[mb], lat.at[rows_of(mb, dp)], load_sem.at[3 + mb]),
            pltpu.make_async_copy(cot_in.at[mb], cot.at[rows_of(mb, dp)], load_sem.at[5 + mb]),
        ]
    own_copies.append(pltpu.make_async_copy(lse_in, lse.at[dp], load_sem.at[7]))
    for c in own_copies:
        c.start()
    mom1_copy.start()
    mom2_copy.start()

    book_copy.wait()

    def make_table(i, _):
        at = pl.ds(aligned(i * 256, 256), 256)
        t = book[at, :].astype(BF16)
        tab[at, :] = t
        tab_t[:, at] = t.T
        wide = t.astype(F32)
        tab4[at, :] = (wide * sharpness).astype(BF16)
        squares = jnp.sum(wide * wide, axis=1, keepdims=True) * (0.5 * sharpness * LOG2E)
        bias[at, :] = jnp.broadcast_to(squares, (256, 128))
        col_sum[at, :] = jnp.zeros((256, 128), F32)
        return 0

    lax.fori_loop(0, CODES // 256, make_table, 0)

    for c in own_copies:
        c.wait()

    def pass_one(mb, owner):
        at = rows_of(mb, owner)
        rows_lat, rows_cot = lat[at, :], cot[at, :]
        shift = lse[owner, 0:1, mb * ROWS : (mb + 1) * ROWS] * LOG2E
        step = 256
        total = jnp.zeros((8, ROWS), F32)
        for k in range(0, CODES, step):
            t = tab4[k : k + step, :]
            b = bias[k : k + step, :]
            logits = dot_nt(t, rows_lat)
            inner = dot_nt(t, rows_cot)
            w = jnp.exp2(logits * LOG2E - jnp.concatenate([b, b], axis=1) - shift)
            total = total + jnp.sum((w * inner).reshape(step // 8, 8, ROWS), axis=0)
            weights[k : k + step, at] = w.astype(BF16)
            dots[k : k + step, at] = inner
        row = jnp.sum(total, axis=0, keepdims=True)
        part[mb, pl.ds(owner * 2, 1), :] = row[:, :128]
        part[mb, pl.ds(owner * 2 + 1, 1), :] = row[:, 128:]


    pass_one(0, dp)
    pass_one(1, dp)

    pl.semaphore_wait(barrier, 38)

    def remote(src, dst, send, recv, to):
        return pltpu.make_async_remote_copy(
            src_ref=src, dst_ref=dst, send_sem=send, recv_sem=recv, device_id=to, device_id_type=MESH
        )

    def row_copies(owner, sends, recvs, to):
        copies = [remote(lse.at[owner], lse.at[owner], sends.at[4], recvs.at[4], to)]
        for mb in range(2):
            at = rows_of(mb, owner)
            copies.append(remote(lat.at[at], lat.at[at], sends.at[2 * mb], recvs.at[2 * mb], to))
            copies.append(remote(cot.at[at], cot.at[at], sends.at[2 * mb + 1], recvs.at[2 * mb + 1], to))
        return copies

    to_partner = row_copies(dp, cs_sem, cr_sem, partner)
    to_y = row_copies(dp, gs_sem, gr_sem, device(x, y + 1 - 2 * core, z, core))
    for c in to_y + to_partner:
        c.start()

    other = (1 - y_lo) * 2 + core
    forward = row_copies(other, fs_sem, fr_sem, partner)
    mate = y_lo * 2 + 1 - core
    other_mate = (1 - y_lo) * 2 + 1 - core

    for i in range(3):
        to_partner[i].wait_recv()
    pass_one(0, mate)
    for i in range(3):
        to_y[i].wait_recv()
        forward[i].start()
    for i in range(3, 5):
        to_partner[i].wait_recv()
    pass_one(1, mate)
    pass_one(0, other)
    for i in range(3, 5):
        to_y[i].wait_recv()
        forward[i].start()
    for i in range(3):
        forward[i].wait_recv()
    pass_one(0, other_mate)

    def ratio_y(mb):
        return [
            remote(part.at[mb], part_y.at[mb, i], ays_sem.at[mb, i], ayr_sem.at[mb, i], yc_peer(i))
            for i in range(1, 8)
        ]

    def ratio_xz(mb):
        return [
            remote(part_s.at[mb], part_xz.at[mb, i], axs_sem.at[mb, i], axr_sem.at[mb, i], xz_peer(i))
            for i in range(1, 16)
        ]

    ry, rx = [ratio_y(0), ratio_y(1)], [ratio_xz(0), ratio_xz(1)]

    def ratio_first(mb):
        for c in ry[mb]:
            c.start()

    def ratio_second(mb):
        for c in ry[mb]:
            c.wait()
        part_s[mb] = part[mb] + jnp.sum(part_y[mb, 1:8], axis=0)
        for c in rx[mb]:
            c.start()

    def ratio_end(mb):
        for c in rx[mb]:
            c.wait()
        ratio[mb] = part_s[mb] + jnp.sum(part_xz[mb, 1:16], axis=0)

    ratio_first(0)
    pass_one(1, other)
    for i in range(3, 5):
        forward[i].wait_recv()
    ratio_second(0)
    pass_one(1, other_mate)
    ratio_first(1)

    def grads_weights(i, _):
        at = pl.ds(aligned(i * 256, 256), 256)
        grads[at, :] = dot(weights[at, :], cot[...])
        return 0

    lax.fori_loop(0, 4, grads_weights, 0)
    ratio_second(1)
    lax.fori_loop(4, 8, grads_weights, 0)

    def scale(mb, u):
        at = pl.ds(aligned(mb * BATCH + u * ROWS, ROWS), ROWS)
        r = jnp.concatenate([ratio[mb, pl.ds(u * 2, 1), :], ratio[mb, pl.ds(u * 2 + 1, 1), :]], axis=1)
        step = 256
        for k in range(0, CODES, step):
            s = weights[k : k + step, at].astype(F32) * (dots[k : k + step, at] - r)
            scaled[k : k + step, at] = s.astype(BF16)
            col_sum[k : k + step, :] += s[:, :128] + s[:, 128:]

    def latent(mb, u):
        at = pl.ds(aligned(mb * BATCH + u * ROWS, ROWS), ROWS)
        lg_part[mb, u] = dot(tab_t[...], scaled[:, at]).astype(BF16)

    def second_pass(mb):
        scale(mb, 0)

        def step(u, _):
            scale(mb, u)
            latent(mb, u - 1)
            return 0

        lax.fori_loop(1, 4, step, 0)
        latent(mb, 3)

    l_core = [
        [
            remote(lg_part.at[mb, h * 2 + 1 - core], lg_core.at[mb, h], lcs_sem.at[mb, h], lcr_sem.at[mb, h], partner)
            for h in range(2)
        ]
        for mb in range(2)
    ]

    def l_y_copy(mb, i):
        to_y_no = (y + i) % 4
        src = lg_pair.at[mb, to_y_no % 2, pl.ds(aligned((to_y_no // 2) * 128, 128), 128)]
        return remote(src, lg_y.at[mb, i], lys_sem.at[mb, i], lyr_sem.at[mb, i], device(x, y + i, z, core))

    l_y = [[l_y_copy(mb, i) for i in range(1, 4)] for mb in range(2)]

    def piece(no):
        return pl.ds(aligned((no // 2) * 16, 16), 16), pl.ds(aligned((no % 2) * 128, 128), 128)

    def l_xz_copy(mb, i):
        to_no = ((x + i // 4) % 4) * 4 + (z + i) % 4
        r, c = piece(to_no)
        return remote(lg_half.at[mb, r, c], lg_xz.at[mb, i], lxs_sem.at[mb, i], lxr_sem.at[mb, i], xz_peer(i))

    def final_place(mb):
        r, c = piece(part_no)
        return lg_all.at[mb, pl.ds(aligned(y_hi * 128 + (part_no // 2) * 16, 16), 16), c]

    def l_all_copy(mb, i):
        return remote(lg_final.at[mb], final_place(mb), lgs_sem.at[mb, i], lgr_sem.at[mb, i], code_peer(i))

    l_xz = [[l_xz_copy(mb, i) for i in range(1, 16)] for mb in range(2)]
    l_all = [[l_all_copy(mb, i) for i in range(1, 32)] for mb in range(2)]

    def latent_0(mb):
        for c in l_core[mb]:
            c.start()

    def latent_1(mb):
        for c in l_core[mb]:
            c.wait()
        for h in range(2):
            lg_pair[mb, h] = (lg_part[mb, h * 2 + core].astype(F32) + lg_core[mb, h].astype(F32)).astype(BF16)
        for c in l_y[mb]:
            c.start()

    def latent_2(mb):
        for c in l_y[mb]:
            c.wait()
        total = lg_pair[mb, y_lo, pl.ds(aligned(y_hi * 128, 128), 128), :].astype(F32)
        for i in range(1, 4):
            total = total + lg_y[mb, i].astype(F32)
        lg_half[mb] = total.astype(BF16)
        for c in l_xz[mb]:
            c.start()

    def latent_3(mb):
        for c in l_xz[mb]:
            c.wait()
        r, c = piece(part_no)
        total = lg_half[mb, r, c].astype(F32)
        for i in range(1, 16):
            total = total + lg_xz[mb, i].astype(F32)
        lg_final[mb] = total.astype(BF16)
        final_place(mb)[...] = total.astype(BF16)
        for c in l_all[mb]:
            c.start()

    def latent_4(mb):
        for c in l_all[mb]:
            c.wait()
        lg_out[mb] = lg_all[mb].T

    def adam(i, _):
        at = pl.ds(aligned(i * 256, 256), 256)
        t = tab[at, :].astype(F32)
        sums = jnp.sum(col_sum[at, :], axis=1, keepdims=True)
        grad = grads[at, :] + dot(scaled[at, :], lat[...]) - sums * t
        new_first = first_decay * mom1[at, :] + (1.0 - first_decay) * grad
        new_second = second_decay * mom2[at, :] + (1.0 - second_decay) * grad * grad
        first_hat = new_first * (1.0 / (1.0 - first_decay**ADAM_STEPS))
        second_hat = new_second * (1.0 / (1.0 - second_decay**ADAM_STEPS))
        code_out[at, :] = book[at, :] - step_rate * first_hat / (jnp.sqrt(second_hat) + epsilon)
        first_out[at, :] = new_first
        second_out[at, :] = new_second
        return 0

    ratio_end(0)
    second_pass(0)
    latent_0(0)
    ratio_end(1)
    second_pass(1)
    latent_0(1)
    latent_1(0)
    mom1_copy.wait()
    mom2_copy.wait()
    lax.fori_loop(0, 1, adam, 0)
    latent_1(1)
    lax.fori_loop(1, 2, adam, 0)
    latent_2(0)
    lax.fori_loop(2, 4, adam, 0)
    latent_2(1)
    lax.fori_loop(4, 5, adam, 0)
    latent_3(0)
    lax.fori_loop(5, 8, adam, 0)
    latent_3(1)
    latent_4(0)
    latent_4(1)
    for c in to_y + to_partner + forward:
        c.wait_send()


def body(latents, cotangent, saved_lse, codebook, first_moment, second_moment):
    lse_rows = jnp.broadcast_to(saved_lse.reshape(1, 2 * ROWS), (8, 2 * ROWS))
    dma = pltpu.SemaphoreType.DMA
    any_spec, vmem_spec = pl.BlockSpec(memory_space=pl.ANY), pl.BlockSpec(memory_space=pltpu.VMEM)
    code_array = jax.ShapeDtypeStruct((CODES, WIDTH), F32)
    lg, new_code, new_first, new_second = pl.pallas_call(
        kernel,
        name="soft_codebook",
        out_shape=(jax.ShapeDtypeStruct((2, ROWS, WIDTH), BF16), code_array, code_array, code_array),
        in_specs=[any_spec] * 6,
        out_specs=[vmem_spec] * 4,
        scratch_shapes=[
            pltpu.VMEM((ALL, WIDTH), BF16),
            pltpu.VMEM((ALL, WIDTH), BF16),
            pltpu.VMEM((4, 8, 2 * ROWS), F32),
            pltpu.VMEM((CODES, WIDTH), F32),
            pltpu.VMEM((CODES, WIDTH), F32),
            pltpu.VMEM((CODES, WIDTH), F32),
            pltpu.VMEM((CODES, WIDTH), BF16),
            pltpu.VMEM((WIDTH, CODES), BF16),
            pltpu.VMEM((CODES, WIDTH), BF16),
            pltpu.VMEM((CODES, 128), F32),
            pltpu.VMEM((CODES, ALL), BF16),
            pltpu.VMEM((CODES, ALL), F32),
            pltpu.VMEM((CODES, ALL), BF16),
            pltpu.VMEM((CODES, WIDTH), F32),
            pltpu.VMEM((CODES, 128), F32),
            pltpu.VMEM((2, 8, 128), F32),
            pltpu.VMEM((2, 8, 8, 128), F32),
            pltpu.VMEM((2, 8, 128), F32),
            pltpu.VMEM((2, 16, 8, 128), F32),
            pltpu.VMEM((2, 8, 128), F32),
            pltpu.VMEM((2, 4, WIDTH, ROWS), BF16),
            pltpu.VMEM((2, 2, WIDTH, ROWS), BF16),
            pltpu.VMEM((2, 2, WIDTH, ROWS), BF16),
            pltpu.VMEM((2, 4, WIDTH // 2, ROWS), BF16),
            pltpu.VMEM((2, WIDTH // 2, ROWS), BF16),
            pltpu.VMEM((2, 16, 16, 128), BF16),
            pltpu.VMEM((2, 16, 128), BF16),
            pltpu.VMEM((2, WIDTH, ROWS), BF16),
            dma((8,)),
            dma((5,)), dma((5,)), dma((5,)), dma((5,)), dma((5,)), dma((5,)),
            dma((2, 8)), dma((2, 8)), dma((2, 16)), dma((2, 16)),
            dma((2, 2)), dma((2, 2)), dma((2, 4)), dma((2, 4)), dma((2, 16)), dma((2, 16)), dma((2, 32)), dma((2, 32)),
        ],
        compiler_params=pltpu.CompilerParams(
            collective_id=0, has_side_effects=True, vmem_limit_bytes=60 * 1024 * 1024
        ),
    )(latents, cotangent, lse_rows, codebook, first_moment, second_moment)
    return lg, new_code, new_first, new_second


def solution(mesh):
    rows, codes = P(None, "dp", None), P(("dp", "code"), None)
    return jax.shard_map(
        body,
        mesh=mesh,
        in_specs=(rows, rows, P(None, "dp"), codes, codes, codes),
        out_specs=(rows, codes, codes, codes),
        check_vma=False,
    )
```

```python
import functools
import math

import jax
import jax.numpy as jnp
from jax import lax
from jax.experimental import pallas as pl
from jax.experimental.pallas import tpu as pltpu
from jax.sharding import PartitionSpec as P

MESH = pl.DeviceIdType.MESH
ADAM_STEPS = 10
sharpness = 0.25
first_decay = 0.5
second_decay = 0.9
step_rate = 0.01
epsilon = 1e-8

LOG2E = math.log2(math.e)
CODES = 2048
WIDTH = 256
ROWS = 256
BATCH = 1024
ALL = 2 * BATCH
F32, BF16 = jnp.float32, jnp.bfloat16


def place():
    dp, code = lax.axis_index("dp"), lax.axis_index("code")
    return code // 8, ((code // 4) % 2) * 2 + dp // 2, code % 4, dp % 2


def device(x, y, z, core):
    x, y, z, core = x % 4, y % 4, z % 4, core % 2
    return ((y % 2) * 2 + core, x * 8 + (y // 2) * 4 + z)


def dot_nt(a, b):
    return lax.dot_general(a, b, (((1,), (1,)), ((), ())), preferred_element_type=F32)


def dot(a, b):
    return jnp.dot(a, b, preferred_element_type=F32)


def aligned(v, n):
    return pl.multiple_of(v, n)


def kernel(
    lat_in, cot_in, lse_in, code_in, first_in, second_in,
    lg_out, code_out, first_out, second_out,
    lat, cot, lse, tab, tab_t, bias, weights, dots, grads, col_sum,
    part, part_y, part_s, part_xz, ratio,
    lg_part, lg_core, lg_pair, lg_y, lg_half, lg_xz, lg_final, lg_all, hop_sem,
    load_sem, gs_sem, gr_sem, fs_sem, fr_sem, cs_sem, cr_sem,
    ays_sem, ayr_sem, axs_sem, axr_sem,
    lcs_sem, lcr_sem, lys_sem, lyr_sem, lxs_sem, lxr_sem, lgs_sem, lgr_sem,
):
    x, y, z, core = place()
    y_lo, y_hi = y % 2, y // 2
    dp = y_lo * 2 + core
    part_no = x * 4 + z
    partner = device(x, y, z, core + 1)

    barrier = pltpu.get_barrier_semaphore()
    along = {
        "core": [partner],
        "x": [device(x + 1, y, z, core), device(x + 3, y, z, core)],
        "y": [device(x, y + 1, z, core), device(x, y + 3, z, core)],
        "z": [device(x, y, z + 1, core), device(x, y, z + 3, core)],
    }
    for peers in along.values():
        for to in peers:
            pl.semaphore_signal(barrier, inc=1, device_id=to, device_id_type=MESH)

    def hear_send(no, axis):
        for to in along[axis]:
            pl.semaphore_signal(hop_sem.at[no], inc=1, device_id=to, device_id_type=MESH)

    def hear_wait(no, axis):
        pl.semaphore_wait(hop_sem.at[no], len(along[axis]))

    def yc_peer(i):
        return device(x, y + i // 2, z, core + i)

    def xz_peer(i):
        return device(x + i // 4, y, z + i, core)

    def code_peer(i):
        return device(x + i // 4, y + (i // 16) * 2, z + i, core)

    book_copy = pltpu.make_async_copy(code_in, code_out, load_sem.at[0])
    mom1_copy = pltpu.make_async_copy(first_in, first_out, load_sem.at[1])
    mom2_copy = pltpu.make_async_copy(second_in, second_out, load_sem.at[2])

    def rows_of(mb, owner):
        return pl.ds(aligned(mb * BATCH + owner * ROWS, ROWS), ROWS)

    own_copies = []
    for mb in range(2):
        own_copies += [
            pltpu.make_async_copy(lat_in.at[mb], lat.at[rows_of(mb, dp)], load_sem.at[3 + mb]),
            pltpu.make_async_copy(cot_in.at[mb], cot.at[rows_of(mb, dp)], load_sem.at[5 + mb]),
        ]
    own_copies.append(pltpu.make_async_copy(lse_in, lse.at[dp], load_sem.at[7]))
    for c in own_copies:
        c.start()
    book_copy.start()
    mom1_copy.start()
    mom2_copy.start()

    def remote(src, dst, send, recv, to):
        return pltpu.make_async_remote_copy(
            src_ref=src, dst_ref=dst, send_sem=send, recv_sem=recv, device_id=to, device_id_type=MESH
        )

    def row_copies(owner, sends, recvs, to):
        copies = [remote(lse.at[owner], lse.at[owner], sends.at[4], recvs.at[4], to)]
        for mb in range(2):
            at = rows_of(mb, owner)
            copies.append(remote(lat.at[at], lat.at[at], sends.at[2 * mb], recvs.at[2 * mb], to))
            copies.append(remote(cot.at[at], cot.at[at], sends.at[2 * mb + 1], recvs.at[2 * mb + 1], to))
        return copies

    to_partner = row_copies(dp, cs_sem, cr_sem, partner)
    to_y = row_copies(dp, gs_sem, gr_sem, device(x, y + 1 - 2 * core, z, core))
    pl.semaphore_wait(barrier, 7)
    for c in own_copies:
        c.wait()
    for c in to_y + to_partner:
        c.start()
    hear_send(0, "y")

    book_copy.wait()

    def make_table(i, _):
        at = pl.ds(aligned(i * 256, 256), 256)
        t = code_out[at, :].astype(BF16)
        tab[at, :] = t
        tab_t[:, at] = t.T
        wide = t.astype(F32)
        squares = jnp.sum(wide * wide, axis=1, keepdims=True) * (0.5 * sharpness * LOG2E)
        bias[at, :] = jnp.broadcast_to(squares, (256, 128))
        return 0

    lax.fori_loop(0, CODES // 256, make_table, 0)

    def pass_one(pairs):
        places = [rows_of(mb, owner) for mb, owner in pairs]
        shifts = [lse[owner, mb : mb + 1, :] * LOG2E for mb, owner in pairs]
        totals = [jnp.zeros((8, ROWS), F32) for _ in pairs]
        step = 256
        for k in range(0, CODES, step):
            t = tab[k : k + step, :]
            b = bias[k : k + step, :]
            b = jnp.concatenate([b, b], axis=1)
            for i, at in enumerate(places):
                logits = dot_nt(t, lat[at, :])
                inner = dot_nt(t, cot[at, :])
                w = jnp.exp2(logits * (sharpness * LOG2E) - b - shifts[i])
                totals[i] = totals[i] + jnp.sum((w * inner).reshape(step // 8, 8, ROWS), axis=0)
                weights[k : k + step, at] = w.astype(BF16)
                dots[k : k + step, at] = inner
        for (mb, owner), total in zip(pairs, totals):
            row = jnp.sum(total, axis=0, keepdims=True)
            part[mb, pl.ds(owner * 2, 1), :] = row[:, :128]
            part[mb, pl.ds(owner * 2 + 1, 1), :] = row[:, 128:]

    def grads_weights(mb, half, first):
        at = pl.ds(aligned(mb * BATCH + half * 512, 512), 512)
        product = dot(weights[:, at], cot[at, :])
        if first:
            grads[...] = product
        else:
            grads[...] += product

    other = (1 - y_lo) * 2 + core
    forward = row_copies(other, fs_sem, fr_sem, partner)
    mate = y_lo * 2 + 1 - core
    other_mate = (1 - y_lo) * 2 + 1 - core

    def ratio_y(mb):
        return [
            remote(part.at[mb], part_y.at[mb, i], ays_sem.at[mb, i], ayr_sem.at[mb, i], yc_peer(i))
            for i in range(1, 8)
        ]

    def ratio_xz(mb):
        return [
            remote(part_s.at[mb], part_xz.at[mb, i], axs_sem.at[mb, i], axr_sem.at[mb, i], xz_peer(i))
            for i in range(1, 16)
        ]

    ry, rx = [ratio_y(0), ratio_y(1)], [ratio_xz(0), ratio_xz(1)]

    def ratio_first(mb):
        for c in ry[mb]:
            c.start()

    def ratio_second(mb):
        for c in ry[mb]:
            c.wait()
        part_s[mb] = part[mb] + jnp.sum(part_y[mb, 1:8], axis=0)
        for c in rx[mb]:
            c.start()

    def ratio_end(mb):
        for c in rx[mb]:
            c.wait()
        ratio[mb] = part_s[mb] + jnp.sum(part_xz[mb, 1:16], axis=0)

    pass_one([(0, dp), (1, dp)])
    hear_wait(0, "y")
    hear_send(1, "core")
    for c in to_partner:
        c.wait_recv()
    pass_one([(0, mate), (1, mate)])
    hear_wait(1, "core")
    hear_send(2, "x")
    for c in to_y[:3]:
        c.wait_recv()
    for c in forward[:3]:
        c.start()
    grads_weights(0, y_lo, True)
    hear_wait(2, "x")
    hear_send(3, "x")
    for c in forward[:3]:
        c.wait_recv()
    pass_one([(0, other), (0, other_mate)])
    ratio_first(0)
    hear_wait(3, "x")
    hear_send(4, "z")
    for c in to_y[3:]:
        c.wait_recv()
    for c in forward[3:]:
        c.start()
    pass_one([(1, other)])
    hear_wait(4, "z")
    hear_send(5, "z")
    for c in forward[3:]:
        c.wait_recv()
    pass_one([(1, other_mate)])
    ratio_first(1)
    hear_wait(5, "z")
    ratio_second(0)
    grads_weights(1, y_lo, False)
    ratio_second(1)
    grads_weights(0, 1 - y_lo, False)
    grads_weights(1, 1 - y_lo, False)

    def scale(mb):
        r = [
            jnp.concatenate([ratio[mb, 2 * u : 2 * u + 1, :], ratio[mb, 2 * u + 1 : 2 * u + 2, :]], axis=1)
            for u in range(4)
        ]
        step = 256
        for k in range(0, CODES, step):
            sums = None
            for u in range(4):
                at = slice(mb * BATCH + u * ROWS, mb * BATCH + (u + 1) * ROWS)
                s = weights[k : k + step, at].astype(F32) * (dots[k : k + step, at] - r[u])
                weights[k : k + step, at] = s.astype(BF16)
                half = s[:, :128] + s[:, 128:]
                sums = half if sums is None else sums + half
            if mb == 0:
                col_sum[k : k + step, :] = sums
            else:
                col_sum[k : k + step, :] += sums

    def latent(mb):
        whole = dot(tab_t[...], weights[:, mb * BATCH : (mb + 1) * BATCH]) * sharpness
        for u in range(4):
            lg_part[mb, u] = whole[:, u * ROWS : (u + 1) * ROWS].astype(BF16)

    def grads_scaled(mb):
        at = slice(mb * BATCH, (mb + 1) * BATCH)
        grads[...] += dot(weights[:, at], lat[at, :]) * sharpness

    l_core = [
        [
            remote(lg_part.at[mb, h * 2 + 1 - core], lg_core.at[mb, h], lcs_sem.at[mb, h], lcr_sem.at[mb, h], partner)
            for h in range(2)
        ]
        for mb in range(2)
    ]

    def l_y_copy(mb, i):
        to_y_no = (y + i) % 4
        src = lg_pair.at[mb, to_y_no % 2, pl.ds(aligned((to_y_no // 2) * 128, 128), 128)]
        return remote(src, lg_y.at[mb, i], lys_sem.at[mb, i], lyr_sem.at[mb, i], device(x, y + i, z, core))

    l_y = [[l_y_copy(mb, i) for i in range(1, 4)] for mb in range(2)]

    def piece(no):
        return pl.ds(aligned((no // 2) * 16, 16), 16), pl.ds(aligned((no % 2) * 128, 128), 128)

    def l_xz_copy(mb, i):
        to_no = ((x + i // 4) % 4) * 4 + (z + i) % 4
        r, c = piece(to_no)
        return remote(lg_half.at[mb, r, c], lg_xz.at[mb, i], lxs_sem.at[mb, i], lxr_sem.at[mb, i], xz_peer(i))

    def final_place(mb):
        r, c = piece(part_no)
        return lg_all.at[mb, pl.ds(aligned(y_hi * 128 + (part_no // 2) * 16, 16), 16), c]

    def l_all_copy(mb, i):
        return remote(lg_final.at[mb], final_place(mb), lgs_sem.at[mb, i], lgr_sem.at[mb, i], code_peer(i))

    l_xz = [[l_xz_copy(mb, i) for i in range(1, 16)] for mb in range(2)]
    l_all = [[l_all_copy(mb, i) for i in range(1, 32)] for mb in range(2)]

    def latent_0(mb):
        for c in l_core[mb]:
            c.start()

    def latent_1(mb):
        for c in l_core[mb]:
            c.wait()
        for h in range(2):
            lg_pair[mb, h] = (lg_part[mb, h * 2 + core].astype(F32) + lg_core[mb, h].astype(F32)).astype(BF16)
        for c in l_y[mb]:
            c.start()

    def latent_2(mb):
        for c in l_y[mb]:
            c.wait()
        total = lg_pair[mb, y_lo, pl.ds(aligned(y_hi * 128, 128), 128), :].astype(F32)
        for i in range(1, 4):
            total = total + lg_y[mb, i].astype(F32)
        lg_half[mb] = total.astype(BF16)
        for c in l_xz[mb]:
            c.start()

    def latent_3(mb):
        for c in l_xz[mb]:
            c.wait()
        r, c = piece(part_no)
        total = lg_half[mb, r, c].astype(F32)
        for i in range(1, 16):
            total = total + lg_xz[mb, i].astype(F32)
        lg_final[mb] = total.astype(BF16)
        final_place(mb)[...] = total.astype(BF16)
        for c in l_all[mb]:
            c.start()

    def latent_4(mb):
        for c in l_all[mb]:
            c.wait()
        lg_out[mb] = lg_all[mb]

    def adam(i, _):
        at = pl.ds(aligned(i * 256, 256), 256)
        t = tab[at, :].astype(F32)
        sums = jnp.sum(col_sum[at, :], axis=1, keepdims=True) * sharpness
        grad = grads[at, :] - sums * t
        new_first = first_decay * first_out[at, :] + (1.0 - first_decay) * grad
        new_second = second_decay * second_out[at, :] + (1.0 - second_decay) * grad * grad
        first_hat = new_first * (1.0 / (1.0 - first_decay**ADAM_STEPS))
        second_hat = new_second * (1.0 / (1.0 - second_decay**ADAM_STEPS))
        code_out[at, :] = code_out[at, :] - step_rate * first_hat / (jnp.sqrt(second_hat) + epsilon)
        first_out[at, :] = new_first
        second_out[at, :] = new_second
        return 0

    ratio_end(0)
    scale(0)
    latent(0)
    latent_0(0)
    ratio_end(1)
    scale(1)
    latent_1(0)
    latent(1)
    latent_0(1)
    grads_scaled(0)
    latent_1(1)
    latent_2(0)
    grads_scaled(1)
    mom1_copy.wait()
    mom2_copy.wait()
    lax.fori_loop(0, 2, adam, 0)
    latent_2(1)
    lax.fori_loop(2, 5, adam, 0)
    latent_3(0)
    lax.fori_loop(5, 8, adam, 0)
    latent_3(1)
    latent_4(0)
    latent_4(1)
    for c in to_y + to_partner + forward:
        c.wait_send()


def write_out(lg_in, code_in, first_in, second_in, lg_out, code_out, first_out, second_out, sems):
    copies = [
        pltpu.make_async_copy(src, dst, sems.at[i])
        for i, (src, dst) in enumerate([(code_in, code_out), (first_in, first_out), (second_in, second_out)])
    ]
    for c in copies:
        c.start()
    for mb in range(2):
        lg_out[mb] = lg_in[mb].T
    for c in copies:
        c.wait()


def body(*arrays):
    dma = pltpu.SemaphoreType.DMA
    any_spec, vmem_spec = pl.BlockSpec(memory_space=pl.ANY), pl.BlockSpec(memory_space=pltpu.VMEM)
    code_shape, rows_shape = (CODES, WIDTH), (2, ROWS, WIDTH)
    parts = pl.pallas_call(
        kernel,
        name="soft_codebook",
        out_shape=(pltpu.VMEM((2, WIDTH, ROWS), BF16),) + (pltpu.VMEM(code_shape, F32),) * 3,
        in_specs=[pl.BlockSpec(memory_space=pltpu.HBM)] * 6,
        out_specs=[vmem_spec] * 4,
        scratch_shapes=[
            pltpu.VMEM((ALL, WIDTH), BF16),
            pltpu.VMEM((ALL, WIDTH), BF16),
            pltpu.VMEM((4, 2, ROWS), F32),
            pltpu.VMEM((CODES, WIDTH), BF16),
            pltpu.VMEM((WIDTH, CODES), BF16),
            pltpu.VMEM((CODES, 128), F32),
            pltpu.VMEM((CODES, ALL), BF16),
            pltpu.VMEM((CODES, ALL), F32),
            pltpu.VMEM((CODES, WIDTH), F32),
            pltpu.VMEM((CODES, 128), F32),
            pltpu.VMEM((2, 8, 128), F32),
            pltpu.VMEM((2, 8, 8, 128), F32),
            pltpu.VMEM((2, 8, 128), F32),
            pltpu.VMEM((2, 16, 8, 128), F32),
            pltpu.VMEM((2, 8, 128), F32),
            pltpu.VMEM((2, 4, WIDTH, ROWS), BF16),
            pltpu.VMEM((2, 2, WIDTH, ROWS), BF16),
            pltpu.VMEM((2, 2, WIDTH, ROWS), BF16),
            pltpu.VMEM((2, 4, WIDTH // 2, ROWS), BF16),
            pltpu.VMEM((2, WIDTH // 2, ROWS), BF16),
            pltpu.VMEM((2, 16, 16, 128), BF16),
            pltpu.VMEM((2, 16, 128), BF16),
            pltpu.VMEM((2, WIDTH, ROWS), BF16),
            pltpu.SemaphoreType.REGULAR((6,)),
            dma((8,)),
            dma((5,)), dma((5,)), dma((5,)), dma((5,)), dma((5,)), dma((5,)),
            dma((2, 8)), dma((2, 8)), dma((2, 16)), dma((2, 16)),
            dma((2, 2)), dma((2, 2)), dma((2, 4)), dma((2, 4)), dma((2, 16)), dma((2, 16)), dma((2, 32)), dma((2, 32)),
        ],
        compiler_params=pltpu.CompilerParams(
            collective_id=0, has_side_effects=True, vmem_limit_bytes=40 * 1024 * 1024
        ),
    )(*[pltpu.with_memory_space_constraint(a, pltpu.HBM) for a in arrays])
    code_array = jax.ShapeDtypeStruct(code_shape, F32)
    return pl.pallas_call(
        write_out,
        name="write_out",
        out_shape=(jax.ShapeDtypeStruct(rows_shape, BF16), code_array, code_array, code_array),
        in_specs=[vmem_spec] * 4,
        out_specs=[vmem_spec] + [any_spec] * 3,
        scratch_shapes=[dma((3,))],
        compiler_params=pltpu.CompilerParams(vmem_limit_bytes=8 * 1024 * 1024),
    )(*[pltpu.with_memory_space_constraint(p, pltpu.VMEM) for p in parts])


def solution(mesh):
    rows, codes = P(None, "dp", None), P(("dp", "code"), None)
    return jax.shard_map(
        body,
        mesh=mesh,
        in_specs=(rows, rows, P(None, "dp"), codes, codes, codes),
        out_specs=(rows, codes, codes, codes),
        check_vma=False,
    )
```

```python
import functools
import math

import jax
import jax.numpy as jnp
from jax import lax
from jax.experimental import pallas as pl
from jax.experimental.pallas import tpu as pltpu
from jax.sharding import PartitionSpec as P

MESH = pl.DeviceIdType.MESH
ADAM_STEPS = 10
sharpness = 0.25
first_decay = 0.5
second_decay = 0.9
step_rate = 0.01
epsilon = 1e-8

LOG2E = math.log2(math.e)
CODES = 2048
WIDTH = 256
ROWS = 256
BATCH = 1024
ALL = 2 * BATCH
F32, BF16 = jnp.float32, jnp.bfloat16


def place():
    dp, code = lax.axis_index("dp"), lax.axis_index("code")
    return code // 8, ((code // 4) % 2) * 2 + dp // 2, code % 4, dp % 2


def device(x, y, z, core):
    x, y, z, core = x % 4, y % 4, z % 4, core % 2
    return ((y % 2) * 2 + core, x * 8 + (y // 2) * 4 + z)


def dot_nt(a, b):
    return lax.dot_general(a, b, (((1,), (1,)), ((), ())), preferred_element_type=F32)


def dot(a, b):
    return jnp.dot(a, b, preferred_element_type=F32)


def aligned(v, n):
    return pl.multiple_of(v, n)


def kernel(
    lat_in, cot_in, lse_in, code_in, first_in, second_in,
    lg_out, code_out, first_out, second_out,
    lat, lat_scaled, cot, lse, tab, tab_t, bias, weights, dots, grads, col_sum,
    part, part_y, part_s, part_xz, ratio,
    lg_part, lg_core, lg_pair, lg_sum, lg_final, lg_all, hop_sem,
    load_sem, gs_sem, gr_sem, fs_sem, fr_sem, cs_sem, cr_sem,
    ays_sem, ayr_sem, axs_sem, axr_sem,
    lcs_sem, lcr_sem, lxs_sem, lxr_sem, lgs_sem, lgr_sem,
):
    x, y, z, core = place()
    y_lo, y_hi = y % 2, y // 2
    dp = y_lo * 2 + core
    part_no = x * 4 + z
    partner = device(x, y, z, core + 1)

    barrier = pltpu.get_barrier_semaphore()
    along = {
        "core": [partner],
        "x": [device(x + 1, y, z, core), device(x + 3, y, z, core)],
        "y": [device(x, y + 1, z, core), device(x, y + 3, z, core)],
        "z": [device(x, y, z + 1, core), device(x, y, z + 3, core)],
    }
    for peers in along.values():
        for to in peers:
            pl.semaphore_signal(barrier, inc=1, device_id=to, device_id_type=MESH)

    def hear_send(no, axis):
        for to in along[axis]:
            pl.semaphore_signal(hop_sem.at[no], inc=1, device_id=to, device_id_type=MESH)

    def hear_wait(no, axis):
        pl.semaphore_wait(hop_sem.at[no], len(along[axis]))

    def yc_peer(i):
        return device(x, y + i // 2, z, core + i)

    def xz_peer(i):
        return device(x + i // 4, y, z + i, core)

    def code_peer(i):
        return device(x + i // 4, y + (i // 16) * 2, z + i, core)

    book_copy = pltpu.make_async_copy(code_in, code_out, load_sem.at[0])
    mom1_copy = pltpu.make_async_copy(first_in, first_out, load_sem.at[1])
    mom2_copy = pltpu.make_async_copy(second_in, second_out, load_sem.at[2])

    def rows_of(mb, owner):
        return pl.ds(aligned(mb * BATCH + owner * ROWS, ROWS), ROWS)

    own_copies = []
    for mb in range(2):
        own_copies += [
            pltpu.make_async_copy(lat_in.at[mb], lat.at[rows_of(mb, dp)], load_sem.at[3 + mb]),
            pltpu.make_async_copy(cot_in.at[mb], cot.at[rows_of(mb, dp)], load_sem.at[5 + mb]),
        ]
    own_copies.append(pltpu.make_async_copy(lse_in, lse.at[dp], load_sem.at[7]))
    book_copy.start()
    for c in own_copies:
        c.start()

    def remote(src, dst, send, recv, to):
        return pltpu.make_async_remote_copy(
            src_ref=src, dst_ref=dst, send_sem=send, recv_sem=recv, device_id=to, device_id_type=MESH
        )

    def wait_bytes(ref, sem):
        pltpu.make_async_copy(ref, ref, sem).wait()

    def row_copies(owner, sends, recvs, to):
        copies = [[], []]
        for mb in range(2):
            at = rows_of(mb, owner)
            for ref in (lat, cot):
                copies[mb].append(remote(ref.at[at], ref.at[at], sends.at[mb], recvs.at[mb], to))
        copies[0].append(remote(lse.at[owner], lse.at[owner], sends.at[2], recvs.at[2], to))
        return copies

    def start_rows(copies, mb):
        for c in copies[mb]:
            c.start()

    def wait_rows(sems, mb):
        wait_bytes(lat.at[pl.ds(0, 2 * ROWS)], sems.at[mb])
        if mb == 0:
            wait_bytes(lse.at[0], sems.at[2])

    to_partner = row_copies(dp, cs_sem, cr_sem, partner)
    to_y = row_copies(dp, gs_sem, gr_sem, device(x, y + 1 - 2 * core, z, core))
    pl.semaphore_wait(barrier, 7)
    for c in own_copies:
        c.wait()
    for mb in range(2):
        start_rows(to_y, mb)
        start_rows(to_partner, mb)
    hear_send(0, "y")

    book_copy.wait()

    def make_table(i, _):
        at = pl.ds(aligned(i * 256, 256), 256)
        t = code_out[at, :].astype(BF16)
        tab[at, :] = t
        wide = t.astype(F32)
        tab_t[:, at] = (wide * sharpness).astype(BF16).T
        squares = jnp.sum(wide * wide, axis=1, keepdims=True) * (0.5 * sharpness * LOG2E)
        bias[at, :] = jnp.broadcast_to(squares, (256, 128))
        return 0

    lax.fori_loop(0, CODES // 256, make_table, 0)
    mom1_copy.start()
    mom2_copy.start()

    def pass_one(pairs):
        places = [rows_of(mb, owner) for mb, owner in pairs]
        shifts = [lse[owner, mb : mb + 1, :] * LOG2E for mb, owner in pairs]
        totals = [jnp.zeros((8, ROWS), F32) for _ in pairs]
        step = 256
        for k in range(0, CODES, step):
            t = tab[k : k + step, :]
            b = bias[k : k + step, :]
            b = jnp.concatenate([b, b], axis=1)
            for i, at in enumerate(places):
                logits = dot_nt(t, lat[at, :])
                inner = dot_nt(t, cot[at, :])
                w = jnp.exp2(logits * (sharpness * LOG2E) - b - shifts[i])
                totals[i] = totals[i] + jnp.sum((w * inner).reshape(step // 8, 8, ROWS), axis=0)
                weights[k : k + step, at] = w.astype(BF16)
                dots[k : k + step, at] = inner
        for (mb, owner), total in zip(pairs, totals):
            row = jnp.sum(total, axis=0, keepdims=True)
            part[mb, pl.ds(owner * 2, 1), :] = row[:, :128]
            part[mb, pl.ds(owner * 2 + 1, 1), :] = row[:, 128:]

    def grads_weights(mb, half, first):
        at = pl.ds(aligned(mb * BATCH + half * 512, 512), 512)
        product = dot(weights[:, at], cot[at, :])
        if first:
            grads[...] = product
        else:
            grads[...] += product

    other = (1 - y_lo) * 2 + core
    forward = row_copies(other, fs_sem, fr_sem, partner)
    mate = y_lo * 2 + 1 - core
    other_mate = (1 - y_lo) * 2 + 1 - core

    def ratio_y(mb):
        return [
            remote(part.at[mb], part_y.at[mb, i], ays_sem.at[mb], ayr_sem.at[mb], yc_peer(i))
            for i in range(1, 8)
        ]

    def ratio_xz(mb):
        return [
            remote(part_s.at[mb], part_xz.at[mb, i], axs_sem.at[mb], axr_sem.at[mb], xz_peer(i))
            for i in range(1, 16)
        ]

    ry, rx = [ratio_y(0), ratio_y(1)], [ratio_xz(0), ratio_xz(1)]

    def ratio_first(mb):
        for c in ry[mb]:
            c.start()

    def ratio_second(mb):
        for sem in (ays_sem, ayr_sem):
            wait_bytes(part_y.at[mb, pl.ds(1, 7)], sem.at[mb])
        part_s[mb] = part[mb] + jnp.sum(part_y[mb, 1:8], axis=0)
        for c in rx[mb]:
            c.start()

    def ratio_end(mb):
        for sem in (axs_sem, axr_sem):
            wait_bytes(part_xz.at[mb, pl.ds(1, 15)], sem.at[mb])
        ratio[mb] = part_s[mb] + jnp.sum(part_xz[mb, 1:16], axis=0)

    pass_one([(0, dp), (1, dp)])
    hear_wait(0, "y")
    hear_send(1, "core")
    wait_rows(cr_sem, 0)
    wait_rows(cr_sem, 1)
    pass_one([(0, mate), (1, mate)])
    hear_wait(1, "core")
    hear_send(2, "x")
    grads_weights(0, y_lo, True)
    hear_wait(2, "x")
    hear_send(3, "x")
    wait_rows(gr_sem, 0)
    start_rows(forward, 0)
    pass_one([(0, other)])
    hear_wait(3, "x")
    hear_send(4, "z")
    wait_rows(fr_sem, 0)
    pass_one([(0, other_mate)])
    ratio_first(0)
    hear_wait(4, "z")
    hear_send(5, "z")
    wait_rows(gr_sem, 1)
    start_rows(forward, 1)
    pass_one([(1, other)])
    hear_wait(5, "z")
    wait_rows(fr_sem, 1)
    pass_one([(1, other_mate)])
    ratio_first(1)
    ratio_second(0)
    grads_weights(1, y_lo, False)
    ratio_second(1)
    grads_weights(0, 1 - y_lo, False)
    grads_weights(1, 1 - y_lo, False)
    lat_scaled[...] = (lat[...].astype(F32) * sharpness).astype(BF16)

    def scale(mb, half):
        r = [
            jnp.concatenate([ratio[mb, 2 * u : 2 * u + 1, :], ratio[mb, 2 * u + 1 : 2 * u + 2, :]], axis=1)
            for u in (2 * half, 2 * half + 1)
        ]
        step = 256
        for k in range(0, CODES, step):
            sums = None
            for u in range(2):
                start = mb * BATCH + (2 * half + u) * ROWS
                at = slice(start, start + ROWS)
                s = weights[k : k + step, at].astype(F32) * (dots[k : k + step, at] - r[u])
                weights[k : k + step, at] = s.astype(BF16)
                pair = s[:, :128] + s[:, 128:]
                sums = pair if sums is None else sums + pair
            if mb == 0 and half == 0:
                col_sum[k : k + step, :] = sums
            else:
                col_sum[k : k + step, :] += sums

    def latent(mb, half):
        start = mb * BATCH + half * 512
        product = dot(tab_t[...], weights[:, start : start + 512])
        for u in range(2):
            lg_part[mb, 2 * half + u] = product[:, u * ROWS : (u + 1) * ROWS].astype(BF16)

    def second_pass(mb):
        scale(mb, 0)
        latent(mb, 0)
        scale(mb, 1)
        latent(mb, 1)

    def grads_scaled(mb, half):
        start = mb * BATCH + half * 512
        at = slice(start, start + 512)
        grads[...] += dot(weights[:, at], lat_scaled[at, :])

    l_core = [
        [
            remote(lg_part.at[mb, h * 2 + 1 - core], lg_core.at[mb, h], lcs_sem.at[mb], lcr_sem.at[mb], partner)
            for h in range(2)
        ]
        for mb in range(2)
    ]

    def place_of(no, hi):
        return (
            pl.ds(aligned(hi * 128 + (no // 2) * 16, 16), 16),
            pl.ds(aligned((no % 2) * 128, 128), 128),
        )

    def chip_peer(i):
        return device(x + i // 16, y + (i // 4) % 4, z + i, core)

    def l_sum_copy(mb, i):
        to_y_no = (y + (i // 4) % 4) % 4
        rows, cols = place_of(((x + i // 16) % 4) * 4 + (z + i) % 4, to_y_no // 2)
        src = lg_pair.at[mb, to_y_no % 2, rows, cols]
        return remote(src, lg_sum.at[mb, i], lxs_sem.at[mb], lxr_sem.at[mb], chip_peer(i))

    def final_place(mb):
        rows, cols = place_of(part_no, y_hi)
        return lg_all.at[mb, rows, cols]

    def l_all_copy(mb, i):
        return remote(lg_final.at[mb], final_place(mb), lgs_sem.at[mb], lgr_sem.at[mb], code_peer(i))

    l_sum = [[l_sum_copy(mb, i) for i in range(1, 64)] for mb in range(2)]
    l_all = [[l_all_copy(mb, i) for i in range(1, 32)] for mb in range(2)]

    def latent_0(mb):
        for c in l_core[mb]:
            c.start()

    def latent_1(mb):
        for sem in (lcs_sem, lcr_sem):
            wait_bytes(lg_core.at[mb], sem.at[mb])
        for h in range(2):
            lg_pair[mb, h] = (lg_part[mb, h * 2 + core].astype(F32) + lg_core[mb, h].astype(F32)).astype(BF16)
        rows, cols = place_of(part_no, y_hi)
        lg_sum[mb, 0] = lg_pair[mb, y_lo, rows, cols]
        for c in l_sum[mb]:
            c.start()

    def latent_2(mb):
        for sem in (lxs_sem, lxr_sem):
            wait_bytes(lg_sum.at[mb, pl.ds(1, 63)], sem.at[mb])
        total = jnp.sum(lg_sum[mb].astype(F32), axis=0).astype(BF16)
        lg_final[mb] = total
        final_place(mb)[...] = total
        for c in l_all[mb]:
            c.start()

    def latent_3(mb):
        for sem in (lgs_sem, lgr_sem):
            wait_bytes(lg_sum.at[mb, pl.ds(1, 31)], sem.at[mb])
        lg_out[mb] = lg_all[mb]

    def adam(i, _):
        at = pl.ds(aligned(i * 256, 256), 256)
        t = tab[at, :].astype(F32)
        sums = jnp.sum(col_sum[at, :], axis=1, keepdims=True) * sharpness
        grad = grads[at, :] - sums * t
        new_first = first_decay * first_out[at, :] + (1.0 - first_decay) * grad
        new_second = second_decay * second_out[at, :] + (1.0 - second_decay) * grad * grad
        first_hat = new_first * (1.0 / (1.0 - first_decay**ADAM_STEPS))
        second_hat = new_second * (1.0 / (1.0 - second_decay**ADAM_STEPS))
        code_out[at, :] = code_out[at, :] - step_rate * first_hat / (jnp.sqrt(second_hat) + epsilon)
        first_out[at, :] = new_first
        second_out[at, :] = new_second
        return 0

    ratio_end(0)
    second_pass(0)
    latent_0(0)
    ratio_end(1)
    scale(1, 0)
    latent_1(0)
    latent(1, 0)
    scale(1, 1)
    latent(1, 1)
    latent_0(1)
    grads_scaled(0, 0)
    latent_1(1)
    grads_scaled(0, 1)
    grads_scaled(1, 0)
    grads_scaled(1, 1)
    mom1_copy.wait()
    mom2_copy.wait()
    latent_2(0)
    lax.fori_loop(0, 8, adam, 0)
    latent_2(1)
    latent_3(0)
    latent_3(1)
    for sems in (cs_sem, gs_sem, fs_sem):
        wait_rows(sems, 0)
        wait_rows(sems, 1)


def write_out(lg_in, code_in, first_in, second_in, lg_out, code_out, first_out, second_out, sems):
    copies = [
        pltpu.make_async_copy(src, dst, sems.at[i])
        for i, (src, dst) in enumerate([(code_in, code_out), (first_in, first_out), (second_in, second_out)])
    ]
    for c in copies:
        c.start()
    for mb in range(2):
        lg_out[mb] = lg_in[mb].T
    for c in copies:
        c.wait()


def body(*arrays):
    dma = pltpu.SemaphoreType.DMA
    any_spec, vmem_spec = pl.BlockSpec(memory_space=pl.ANY), pl.BlockSpec(memory_space=pltpu.VMEM)
    code_shape, rows_shape = (CODES, WIDTH), (2, ROWS, WIDTH)
    parts = pl.pallas_call(
        kernel,
        name="soft_codebook",
        out_shape=(pltpu.VMEM((2, WIDTH, ROWS), BF16),) + (pltpu.VMEM(code_shape, F32),) * 3,
        in_specs=[pl.BlockSpec(memory_space=pltpu.HBM)] * 6,
        out_specs=[vmem_spec] * 4,
        scratch_shapes=[
            pltpu.VMEM((ALL, WIDTH), BF16),
            pltpu.VMEM((ALL, WIDTH), BF16),
            pltpu.VMEM((ALL, WIDTH), BF16),
            pltpu.VMEM((4, 2, ROWS), F32),
            pltpu.VMEM((CODES, WIDTH), BF16),
            pltpu.VMEM((WIDTH, CODES), BF16),
            pltpu.VMEM((CODES, 128), F32),
            pltpu.VMEM((CODES, ALL), BF16),
            pltpu.VMEM((CODES, ALL), F32),
            pltpu.VMEM((CODES, WIDTH), F32),
            pltpu.VMEM((CODES, 128), F32),
            pltpu.VMEM((2, 8, 128), F32),
            pltpu.VMEM((2, 8, 8, 128), F32),
            pltpu.VMEM((2, 8, 128), F32),
            pltpu.VMEM((2, 16, 8, 128), F32),
            pltpu.VMEM((2, 8, 128), F32),
            pltpu.VMEM((2, 4, WIDTH, ROWS), BF16),
            pltpu.VMEM((2, 2, WIDTH, ROWS), BF16),
            pltpu.VMEM((2, 2, WIDTH, ROWS), BF16),
            pltpu.VMEM((2, 64, 16, 128), BF16),
            pltpu.VMEM((2, 16, 128), BF16),
            pltpu.VMEM((2, WIDTH, ROWS), BF16),
            pltpu.SemaphoreType.REGULAR((6,)),
            dma((8,)),
            dma((3,)), dma((3,)), dma((3,)), dma((3,)), dma((3,)), dma((3,)),
            dma((2,)), dma((2,)), dma((2,)), dma((2,)),
            dma((2,)), dma((2,)), dma((2,)), dma((2,)), dma((2,)), dma((2,)),
        ],
        compiler_params=pltpu.CompilerParams(
            collective_id=0, has_side_effects=True, vmem_limit_bytes=40 * 1024 * 1024
        ),
    )(*[pltpu.with_memory_space_constraint(a, pltpu.HBM) for a in arrays])
    code_array = jax.ShapeDtypeStruct(code_shape, F32)
    return pl.pallas_call(
        write_out,
        name="write_out",
        out_shape=(jax.ShapeDtypeStruct(rows_shape, BF16), code_array, code_array, code_array),
        in_specs=[vmem_spec] * 4,
        out_specs=[vmem_spec] + [any_spec] * 3,
        scratch_shapes=[dma((3,))],
        compiler_params=pltpu.CompilerParams(vmem_limit_bytes=8 * 1024 * 1024),
    )(*[pltpu.with_memory_space_constraint(p, pltpu.VMEM) for p in parts])


def solution(mesh):
    rows, codes = P(None, "dp", None), P(("dp", "code"), None)
    return jax.shard_map(
        body,
        mesh=mesh,
        in_specs=(rows, rows, P(None, "dp"), codes, codes, codes),
        out_specs=(rows, codes, codes, codes),
        check_vma=False,
    )
```

```python
import functools
import math

import jax
import jax.numpy as jnp
from jax import lax
from jax.experimental import pallas as pl
from jax.experimental.pallas import tpu as pltpu
from jax.sharding import PartitionSpec as P

MESH = pl.DeviceIdType.MESH
ADAM_STEPS = 10
sharpness = 0.25
first_decay = 0.5
second_decay = 0.9
step_rate = 0.01
epsilon = 1e-8

LOG2E = math.log2(math.e)
CODES = 2048
WIDTH = 256
ROWS = 256
BATCH = 1024
ALL = 2 * BATCH
F32, BF16 = jnp.float32, jnp.bfloat16


def place():
    dp, code = lax.axis_index("dp"), lax.axis_index("code")
    return code // 8, ((code // 4) % 2) * 2 + dp // 2, code % 4, dp % 2


def device(x, y, z, core):
    x, y, z, core = x % 4, y % 4, z % 4, core % 2
    return ((y % 2) * 2 + core, x * 8 + (y // 2) * 4 + z)


def dot_nt(a, b):
    return lax.dot_general(a, b, (((1,), (1,)), ((), ())), preferred_element_type=F32)


def dot(a, b):
    return jnp.dot(a, b, preferred_element_type=F32)


def aligned(v, n):
    return pl.multiple_of(v, n)


def kernel(
    lat_in, cot_in, lse_in, code_in, first_in, second_in,
    lg_out, code_out, first_out, second_out,
    lat, cot, lse, tab, tab_t, bias, weights, scaled, dots, grads, col_sum,
    part, part_y, part_s, part_xz, ratio,
    lg_part, lg_core, lg_pair, lg_sum, lg_final, lg_all, hop_sem,
    load_sem, gs_sem, gr_sem, fs_sem, fr_sem, cs_sem, cr_sem,
    ays_sem, ayr_sem, axs_sem, axr_sem,
    lcs_sem, lcr_sem, lxs_sem, lxr_sem, lgs_sem, lgr_sem,
):
    x, y, z, core = place()
    y_lo, y_hi = y % 2, y // 2
    dp = y_lo * 2 + core
    part_no = x * 4 + z
    partner = device(x, y, z, core + 1)

    barrier = pltpu.get_barrier_semaphore()
    along = {
        "core": [partner],
        "x": [device(x + 1, y, z, core), device(x + 3, y, z, core)],
        "y": [device(x, y + 1, z, core), device(x, y + 3, z, core)],
        "z": [device(x, y, z + 1, core), device(x, y, z + 3, core)],
    }
    for peers in along.values():
        for to in peers:
            pl.semaphore_signal(barrier, inc=1, device_id=to, device_id_type=MESH)

    def hear_send(no, axis):
        for to in along[axis]:
            pl.semaphore_signal(hop_sem.at[no], inc=1, device_id=to, device_id_type=MESH)

    def hear_wait(no, axis):
        pl.semaphore_wait(hop_sem.at[no], len(along[axis]))

    def yc_peer(i):
        return device(x, y + i // 2, z, core + i)

    def xz_peer(i):
        return device(x + i // 4, y, z + i, core)

    def code_peer(i):
        return device(x + i // 4, y + (i // 16) * 2, z + i, core)

    book_copy = pltpu.make_async_copy(code_in, code_out, load_sem.at[0])
    mom1_copy = pltpu.make_async_copy(first_in, first_out, load_sem.at[1])
    mom2_copy = pltpu.make_async_copy(second_in, second_out, load_sem.at[2])

    def rows_of(mb, owner):
        return pl.ds(aligned(mb * BATCH + owner * ROWS, ROWS), ROWS)

    own_copies = []
    for mb in range(2):
        own_copies += [
            pltpu.make_async_copy(lat_in.at[mb], lat.at[rows_of(mb, dp)], load_sem.at[3 + mb]),
            pltpu.make_async_copy(cot_in.at[mb], cot.at[rows_of(mb, dp)], load_sem.at[5 + mb]),
        ]
    own_copies.append(pltpu.make_async_copy(lse_in, lse.at[dp], load_sem.at[7]))
    for c in own_copies:
        c.start()
    book_copy.start()

    def remote(src, dst, send, recv, to):
        return pltpu.make_async_remote_copy(
            src_ref=src, dst_ref=dst, send_sem=send, recv_sem=recv, device_id=to, device_id_type=MESH
        )

    def wait_bytes(ref, sem):
        pltpu.make_async_copy(ref, ref, sem).wait()

    def row_copies(owner, sends, recvs, to_lat, to_cot):
        copies = [[], []]
        for mb in range(2):
            at = rows_of(mb, owner)
            for ref, to in ((lat, to_lat), (cot, to_cot)):
                copies[mb].append(remote(ref.at[at], ref.at[at], sends.at[mb], recvs.at[mb], to))
        copies[0].append(remote(lse.at[owner], lse.at[owner], sends.at[2], recvs.at[2], to_lat))
        return copies

    def start_rows(copies, mb):
        for c in copies[mb]:
            c.start()

    def wait_rows(sems, mb):
        wait_bytes(lat.at[pl.ds(0, 2 * ROWS)], sems.at[mb])
        if mb == 0:
            wait_bytes(lse.at[0], sems.at[2])

    to_partner = row_copies(dp, cs_sem, cr_sem, partner, partner)
    to_y = row_copies(dp, gs_sem, gr_sem, device(x, y + 1, z, core), device(x, y + 3, z, core))
    pl.semaphore_wait(barrier, 7)
    for c in own_copies:
        c.wait()
    start_rows(to_y, 0)
    hear_send(0, "y")
    start_rows(to_partner, 0)
    start_rows(to_partner, 1)

    book_copy.wait()
    hear_wait(0, "y")
    hear_send(1, "core")

    def make_table(i, _):
        at = pl.ds(aligned(i * 256, 256), 256)
        t = code_out[at, :].astype(BF16)
        tab[at, :] = t
        wide = t.astype(F32)
        tab_t[:, at] = t.T
        squares = jnp.sum(wide * wide, axis=1, keepdims=True) * (0.5 * sharpness * LOG2E)
        bias[at, :] = jnp.broadcast_to(squares, (256, 128))
        return 0

    lax.fori_loop(0, CODES // 256, make_table, 0)
    start_rows(to_y, 1)
    mom1_copy.start()
    mom2_copy.start()
    hear_wait(1, "core")
    hear_send(2, "x")

    def pass_one(pairs):
        places = [rows_of(mb, owner) for mb, owner in pairs]
        shifts = [lse[owner, mb : mb + 1, :] * LOG2E for mb, owner in pairs]
        totals = [jnp.zeros((8, ROWS), F32) for _ in pairs]
        step = 256
        for k in range(0, CODES, step):
            t = tab[k : k + step, :]
            b = bias[k : k + step, :]
            b = jnp.concatenate([b, b], axis=1)
            for i, at in enumerate(places):
                logits = dot_nt(t, lat[at, :])
                inner = dot_nt(t, cot[at, :]) * sharpness
                w = jnp.exp2(logits * (sharpness * LOG2E) - b - shifts[i])
                totals[i] = totals[i] + jnp.sum((w * inner).reshape(step // 8, 8, ROWS), axis=0)
                weights[k : k + step, at] = w.astype(BF16)
                dots[k : k + step, at] = inner
        for (mb, owner), total in zip(pairs, totals):
            row = jnp.sum(total, axis=0, keepdims=True)
            part[mb, pl.ds(owner * 2, 1), :] = row[:, :128]
            part[mb, pl.ds(owner * 2 + 1, 1), :] = row[:, 128:]

    def grads_weights(mb, half, first):
        at = pl.ds(aligned(mb * BATCH + half * 512, 512), 512)
        product = dot(weights[:, at], cot[at, :])
        if first:
            grads[...] = product
        else:
            grads[...] += product

    other = (1 - y_lo) * 2 + core
    forward = row_copies(other, fs_sem, fr_sem, partner, partner)
    mate = y_lo * 2 + 1 - core
    other_mate = (1 - y_lo) * 2 + 1 - core

    def ratio_y(mb):
        return [
            remote(part.at[mb], part_y.at[mb, i], ays_sem.at[mb], ayr_sem.at[mb], yc_peer(i))
            for i in range(1, 8)
        ]

    def ratio_xz(mb):
        return [
            remote(part_s.at[mb], part_xz.at[mb, i], axs_sem.at[mb], axr_sem.at[mb], xz_peer(i))
            for i in range(1, 16)
        ]

    ry, rx = [ratio_y(0), ratio_y(1)], [ratio_xz(0), ratio_xz(1)]

    def ratio_first(mb):
        for c in ry[mb]:
            c.start()

    def ratio_second(mb):
        for sem in (ays_sem, ayr_sem):
            wait_bytes(part_y.at[mb, pl.ds(1, 7)], sem.at[mb])
        part_s[mb] = part[mb] + jnp.sum(part_y[mb, 1:8], axis=0)
        for c in rx[mb]:
            c.start()

    def ratio_end(mb):
        for sem in (axs_sem, axr_sem):
            wait_bytes(part_xz.at[mb, pl.ds(1, 15)], sem.at[mb])
        ratio[mb] = part_s[mb] + jnp.sum(part_xz[mb, 1:16], axis=0)

    pass_one([(0, dp), (1, dp)])
    hear_wait(2, "x")
    hear_send(3, "x")
    wait_rows(cr_sem, 0)
    wait_rows(cr_sem, 1)
    pass_one([(0, mate), (1, mate)])
    hear_wait(3, "x")
    hear_send(4, "z")
    wait_rows(gr_sem, 0)
    start_rows(forward, 0)
    pass_one([(0, other)])
    hear_wait(4, "z")
    hear_send(5, "z")
    wait_rows(fr_sem, 0)
    pass_one([(0, other_mate)])
    ratio_first(0)
    wait_rows(gr_sem, 1)
    start_rows(forward, 1)
    pass_one([(1, other)])
    hear_wait(5, "z")
    wait_rows(fr_sem, 1)
    pass_one([(1, other_mate)])
    ratio_first(1)
    ratio_second(0)
    grads_weights(0, y_lo, True)
    ratio_second(1)
    grads_weights(1, y_lo, False)

    def scale(mb, half):
        r = [
            jnp.concatenate([ratio[mb, 2 * u : 2 * u + 1, :], ratio[mb, 2 * u + 1 : 2 * u + 2, :]], axis=1)
            for u in (2 * half, 2 * half + 1)
        ]
        step = 256
        for k in range(0, CODES, step):
            sums = None
            for u in range(2):
                start = mb * BATCH + (2 * half + u) * ROWS
                at = slice(start, start + ROWS)
                s = weights[k : k + step, at].astype(F32) * (dots[k : k + step, at] - r[u])
                scaled[k : k + step, at] = s.astype(BF16)
                pair = s[:, :128] + s[:, 128:]
                sums = pair if sums is None else sums + pair
            if mb == 0 and half == 0:
                col_sum[k : k + step, :] = sums
            else:
                col_sum[k : k + step, :] += sums

    def latent(mb, half):
        start = mb * BATCH + half * 512
        product = dot(tab_t[...], scaled[:, start : start + 512])
        for u in range(2):
            lg_part[mb, 2 * half + u] = product[:, u * ROWS : (u + 1) * ROWS].astype(BF16)

    def grads_scaled(mb, half):
        start = mb * BATCH + half * 512
        at = slice(start, start + 512)
        grads[...] += dot(scaled[:, at], lat[at, :])

    l_core = [
        [
            remote(
                lg_part.at[mb, h * 2 + 1 - core], lg_core.at[mb, h], lcs_sem.at[mb, h], lcr_sem.at[mb, h], partner
            )
            for h in range(2)
        ]
        for mb in range(2)
    ]

    def place_of(no, hi):
        return (
            pl.ds(aligned(hi * 128 + (no // 2) * 16, 16), 16),
            pl.ds(aligned((no % 2) * 128, 128), 128),
        )

    own_slot = x * 16 + y * 4 + z

    def l_sum_copy(mb, h, i):
        to_x, to_hi, to_z = (x + i // 8) % 4, (y_hi + (i // 4) % 2) % 2, (z + i) % 4
        rows, cols = place_of(to_x * 4 + to_z, to_hi)
        return remote(
            lg_pair.at[mb, h, rows, cols],
            lg_sum.at[mb, own_slot],
            lxs_sem.at[mb],
            lxr_sem.at[mb],
            device(to_x, to_hi * 2 + h, to_z, core),
        )

    def final_place(mb):
        rows, cols = place_of(part_no, y_hi)
        return lg_all.at[mb, rows, cols]

    def l_all_copy(mb, i):
        return remote(lg_final.at[mb], final_place(mb), lgs_sem.at[mb], lgr_sem.at[mb], code_peer(i))

    l_sum = [[[l_sum_copy(mb, h, i) for i in range(32)] for h in range(2)] for mb in range(2)]
    l_all = [[l_all_copy(mb, i) for i in range(1, 32)] for mb in range(2)]

    def latent_0(mb, h):
        l_core[mb][h].start()

    def latent_1(mb, h):
        for sem in (lcs_sem, lcr_sem):
            wait_bytes(lg_core.at[mb, h], sem.at[mb, h])
        lg_pair[mb, h] = (lg_part[mb, h * 2 + core].astype(F32) + lg_core[mb, h].astype(F32)).astype(BF16)
        for c in l_sum[mb][h][1:]:
            c.start()

        @pl.when(y_lo != h)
        def _():
            l_sum[mb][h][0].start()

        @pl.when(y_lo == h)
        def _():
            rows, cols = place_of(part_no, y_hi)
            lg_sum[mb, own_slot] = lg_pair[mb, h, rows, cols]

    def latent_2(mb):
        for sem in (lxs_sem, lxr_sem):
            wait_bytes(lg_sum.at[mb, pl.ds(0, 63)], sem.at[mb])
        total = jnp.sum(lg_sum[mb].astype(F32), axis=0).astype(BF16)
        lg_final[mb] = total
        final_place(mb)[...] = total
        for c in l_all[mb]:
            c.start()

    def latent_3(mb):
        for sem in (lgs_sem, lgr_sem):
            wait_bytes(lg_sum.at[mb, pl.ds(1, 31)], sem.at[mb])
        lg_out[mb] = lg_all[mb]

    def adam(i, _):
        at = pl.ds(aligned(i * 256, 256), 256)
        t = tab[at, :].astype(F32)
        sums = jnp.sum(col_sum[at, :], axis=1, keepdims=True)
        grad = grads[at, :] - sums * t
        new_first = first_decay * first_out[at, :] + (1.0 - first_decay) * grad
        new_second = second_decay * second_out[at, :] + (1.0 - second_decay) * grad * grad
        first_hat = new_first * (1.0 / (1.0 - first_decay**ADAM_STEPS))
        second_hat = new_second * (1.0 / (1.0 - second_decay**ADAM_STEPS))
        code_out[at, :] = code_out[at, :] - step_rate * first_hat / (jnp.sqrt(second_hat) + epsilon)
        first_out[at, :] = new_first
        second_out[at, :] = new_second
        return 0

    ratio_end(0)
    scale(0, 0)
    latent(0, 0)
    latent_0(0, 0)
    scale(0, 1)
    latent(0, 1)
    latent_0(0, 1)
    latent_1(0, 0)
    ratio_end(1)
    scale(1, 0)
    latent(1, 0)
    latent_0(1, 0)
    latent_1(0, 1)
    scale(1, 1)
    latent(1, 1)
    latent_0(1, 1)
    latent_1(1, 0)
    grads_scaled(0, 0)
    latent_1(1, 1)
    grads_scaled(0, 1)
    grads_scaled(1, 0)
    latent_2(0)
    grads_scaled(1, 1)
    latent_2(1)
    grads_weights(0, 1 - y_lo, False)
    grads_weights(1, 1 - y_lo, False)
    mom1_copy.wait()
    mom2_copy.wait()
    lax.fori_loop(0, 8, adam, 0)
    latent_3(0)
    latent_3(1)
    for sems in (cs_sem, gs_sem, fs_sem):
        wait_rows(sems, 0)
        wait_rows(sems, 1)


def write_out(lg_in, code_in, first_in, second_in, lg_out, code_out, first_out, second_out, sems):
    copies = [
        pltpu.make_async_copy(src, dst, sems.at[i])
        for i, (src, dst) in enumerate([(code_in, code_out), (first_in, first_out), (second_in, second_out)])
    ]
    for c in copies:
        c.start()
    for mb in range(2):
        lg_out[mb] = lg_in[mb].T
    for c in copies:
        c.wait()


def body(*arrays):
    dma = pltpu.SemaphoreType.DMA
    any_spec, vmem_spec = pl.BlockSpec(memory_space=pl.ANY), pl.BlockSpec(memory_space=pltpu.VMEM)
    code_shape, rows_shape = (CODES, WIDTH), (2, ROWS, WIDTH)
    parts = pl.pallas_call(
        kernel,
        name="soft_codebook",
        out_shape=(pltpu.VMEM((2, WIDTH, ROWS), BF16),) + (pltpu.VMEM(code_shape, F32),) * 3,
        in_specs=[pl.BlockSpec(memory_space=pltpu.HBM)] * 6,
        out_specs=[vmem_spec] * 4,
        scratch_shapes=[
            pltpu.VMEM((ALL, WIDTH), BF16),
            pltpu.VMEM((ALL, WIDTH), BF16),
            pltpu.VMEM((4, 2, ROWS), F32),
            pltpu.VMEM((CODES, WIDTH), BF16),
            pltpu.VMEM((WIDTH, CODES), BF16),
            pltpu.VMEM((CODES, 128), F32),
            pltpu.VMEM((CODES, ALL), BF16),
            pltpu.VMEM((CODES, ALL), BF16),
            pltpu.VMEM((CODES, ALL), F32),
            pltpu.VMEM((CODES, WIDTH), F32),
            pltpu.VMEM((CODES, 128), F32),
            pltpu.VMEM((2, 8, 128), F32),
            pltpu.VMEM((2, 8, 8, 128), F32),
            pltpu.VMEM((2, 8, 128), F32),
            pltpu.VMEM((2, 16, 8, 128), F32),
            pltpu.VMEM((2, 8, 128), F32),
            pltpu.VMEM((2, 4, WIDTH, ROWS), BF16),
            pltpu.VMEM((2, 2, WIDTH, ROWS), BF16),
            pltpu.VMEM((2, 2, WIDTH, ROWS), BF16),
            pltpu.VMEM((2, 64, 16, 128), BF16),
            pltpu.VMEM((2, 16, 128), BF16),
            pltpu.VMEM((2, WIDTH, ROWS), BF16),
            pltpu.SemaphoreType.REGULAR((6,)),
            dma((8,)),
            dma((3,)), dma((3,)), dma((3,)), dma((3,)), dma((3,)), dma((3,)),
            dma((2,)), dma((2,)), dma((2,)), dma((2,)),
            dma((2, 2)), dma((2, 2)), dma((2,)), dma((2,)), dma((2,)), dma((2,)),
        ],
        compiler_params=pltpu.CompilerParams(
            collective_id=0, has_side_effects=True, vmem_limit_bytes=47 * 1024 * 1024
        ),
    )(*[pltpu.with_memory_space_constraint(a, pltpu.HBM) for a in arrays])
    code_array = jax.ShapeDtypeStruct(code_shape, F32)
    return pl.pallas_call(
        write_out,
        name="write_out",
        out_shape=(jax.ShapeDtypeStruct(rows_shape, BF16), code_array, code_array, code_array),
        in_specs=[vmem_spec] * 4,
        out_specs=[vmem_spec] + [any_spec] * 3,
        scratch_shapes=[dma((3,))],
        compiler_params=pltpu.CompilerParams(vmem_limit_bytes=8 * 1024 * 1024),
    )(*[pltpu.with_memory_space_constraint(p, pltpu.VMEM) for p in parts])


def solution(mesh):
    rows, codes = P(None, "dp", None), P(("dp", "code"), None)
    return jax.shard_map(
        body,
        mesh=mesh,
        in_specs=(rows, rows, P(None, "dp"), codes, codes, codes),
        out_specs=(rows, codes, codes, codes),
        check_vma=False,
    )
```

```python
import functools
import math

import jax
import jax.numpy as jnp
from jax import lax
from jax.experimental import pallas as pl
from jax.experimental.pallas import tpu as pltpu
from jax.sharding import PartitionSpec as P

MESH = pl.DeviceIdType.MESH
ADAM_STEPS = 10
sharpness = 0.25
first_decay = 0.5
second_decay = 0.9
step_rate = 0.01
epsilon = 1e-8

LOG2E = math.log2(math.e)
CODES = 2048
WIDTH = 256
ROWS = 256
BATCH = 1024
ALL = 2 * BATCH
F32, BF16 = jnp.float32, jnp.bfloat16


def place():
    dp, code = lax.axis_index("dp"), lax.axis_index("code")
    return code // 8, ((code // 4) % 2) * 2 + dp // 2, code % 4, dp % 2


def device(x, y, z, core):
    x, y, z, core = x % 4, y % 4, z % 4, core % 2
    return ((y % 2) * 2 + core, x * 8 + (y // 2) * 4 + z)


def aligned(v, n):
    return pl.multiple_of(v, n)


def kernel(
    acc_grads, acc_work,
    lat_in, cot_in, lse_in, code_in, first_in, second_in,
    lg_out, code_out, first_out, second_out,
    lat, cot, lse, tab, tab_t, bias, weights, scaled, dots, grads, col_sum,
    part, part_y, part_s, part_xz, ratio,
    lg_part, lg_core, lg_pair, lg_sum, lg_final, lg_all, hop_sem,
    load_sem, gs_sem, gr_sem, fs_sem, fr_sem, cs_sem, cr_sem,
    ays_sem, ayr_sem, axs_sem, axr_sem,
    lcs_sem, lcr_sem, lxs_sem, lxr_sem, lgs_sem, lgr_sem,
):
    x, y, z, core = place()
    y_lo, y_hi = y % 2, y // 2
    dp = y_lo * 2 + core
    part_no = x * 4 + z
    partner = device(x, y, z, core + 1)

    barrier = pltpu.get_barrier_semaphore()
    along = {
        "core": [partner],
        "x": [device(x + 1, y, z, core), device(x + 3, y, z, core)],
        "y": [device(x, y + 1, z, core), device(x, y + 3, z, core)],
        "z": [device(x, y, z + 1, core), device(x, y, z + 3, core)],
    }
    for peers in along.values():
        for to in peers:
            pl.semaphore_signal(barrier, inc=1, device_id=to, device_id_type=MESH)

    def hear_send(no, axis):
        for to in along[axis]:
            pl.semaphore_signal(hop_sem.at[no], inc=1, device_id=to, device_id_type=MESH)

    def hear_wait(no, axis):
        pl.semaphore_wait(hop_sem.at[no], len(along[axis]))

    def yc_peer(i):
        return device(x, y + i // 2, z, core + i)

    def xz_peer(i):
        return device(x + i // 4, y, z + i, core)

    def code_peer(i):
        return device(x + i // 4, y + (i // 16) * 2, z + i, core)

    book_copy = pltpu.make_async_copy(code_in, code_out, load_sem.at[0])
    mom1_copy = pltpu.make_async_copy(first_in, first_out, load_sem.at[1])
    mom2_copy = pltpu.make_async_copy(second_in, second_out, load_sem.at[2])

    def rows_of(mb, owner):
        return pl.ds(aligned(mb * BATCH + owner * ROWS, ROWS), ROWS)

    own_copies = []
    for mb in range(2):
        own_copies += [
            pltpu.make_async_copy(lat_in.at[mb], lat.at[rows_of(mb, dp)], load_sem.at[3 + mb]),
            pltpu.make_async_copy(cot_in.at[mb], cot.at[rows_of(mb, dp)], load_sem.at[5 + mb]),
        ]
    own_copies.append(pltpu.make_async_copy(lse_in, lse.at[dp], load_sem.at[7]))
    for c in own_copies:
        c.start()
    book_copy.start()

    def remote(src, dst, send, recv, to):
        return pltpu.make_async_remote_copy(
            src_ref=src, dst_ref=dst, send_sem=send, recv_sem=recv, device_id=to, device_id_type=MESH
        )

    def wait_bytes(ref, sem):
        pltpu.make_async_copy(ref, ref, sem).wait()

    def row_copies(owner, sends, recvs, to_lat, to_cot):
        copies = [[], []]
        for mb in range(2):
            at = rows_of(mb, owner)
            for ref, to in ((lat, to_lat), (cot, to_cot)):
                copies[mb].append(remote(ref.at[at], ref.at[at], sends.at[mb], recvs.at[mb], to))
        copies[0].append(remote(lse.at[owner], lse.at[owner], sends.at[2], recvs.at[2], to_lat))
        return copies

    def start_rows(copies, mb):
        for c in copies[mb]:
            c.start()

    def wait_rows(sems, mb):
        wait_bytes(lat.at[pl.ds(0, 2 * ROWS)], sems.at[mb])
        if mb == 0:
            wait_bytes(lse.at[0], sems.at[2])

    to_partner = row_copies(dp, cs_sem, cr_sem, partner, partner)
    to_y = row_copies(dp, gs_sem, gr_sem, device(x, y + 1, z, core), device(x, y + 3, z, core))
    pl.semaphore_wait(barrier, 7)
    for c in own_copies:
        c.wait()
    start_rows(to_y, 0)
    hear_send(0, "y")
    start_rows(to_partner, 0)
    start_rows(to_partner, 1)

    book_copy.wait()

    def make_table(i, _):
        at = pl.ds(aligned(i * 256, 256), 256)
        t = code_out[at, :].astype(BF16)
        tab[at, :] = t
        wide = t.astype(F32)
        tab_t[:, at] = t.T
        squares = jnp.sum(wide * wide, axis=1, keepdims=True) * (0.5 * sharpness * LOG2E)
        bias[at, :] = jnp.broadcast_to(squares, (256, 128))
        return 0

    lax.fori_loop(0, CODES // 256, make_table, 0)
    start_rows(to_y, 1)
    mom1_copy.start()
    mom2_copy.start()
    hear_wait(0, "y")
    hear_send(1, "core")

    staged = [0, 0]

    def push(rhs, unit, transpose=False):
        staged[unit] = 1 - staged[unit]
        pltpu.matmul_push_rhs(rhs, staged[unit], unit, transpose=transpose)
        return staged[unit]

    def pass_one(pairs):
        places = [rows_of(mb, owner) for mb, owner in pairs]
        shifts = [lse[owner, mb : mb + 1, :] * LOG2E for mb, owner in pairs]
        totals = [jnp.zeros((8, ROWS), F32) for _ in pairs]
        step = 256
        tiles = [(i, k) for i in range(len(pairs)) for k in range(0, CODES, step)]

        def multiply(n):
            i, k = tiles[n]
            for unit, rows in enumerate((lat, cot)):
                load = push(rows[places[i], :], unit, transpose=True) if k == 0 else None
                pltpu.matmul_acc_lhs(acc_work[unit][n % 2], tab[k : k + step, :], load)

        multiply(0)
        for n, (i, k) in enumerate(tiles):
            if n + 1 < len(tiles):
                multiply(n + 1)
            b = bias[k : k + step, :]
            logits = pltpu.matmul_pop(acc_work[0][n % 2])
            inner = pltpu.matmul_pop(acc_work[1][n % 2]) * sharpness
            w = jnp.exp2(logits * (sharpness * LOG2E) - jnp.concatenate([b, b], axis=1) - shifts[i])
            totals[i] = totals[i] + jnp.sum((w * inner).reshape(step // 8, 8, ROWS), axis=0)
            weights[k : k + step, places[i]] = w.astype(BF16)
            dots[k : k + step, places[i]] = inner
        for (mb, owner), total in zip(pairs, totals):
            row = jnp.sum(total, axis=0, keepdims=True)
            part[mb, pl.ds(owner * 2, 1), :] = row[:, :128]
            part[mb, pl.ds(owner * 2 + 1, 1), :] = row[:, 128:]

    def add_grads(terms, half, first=False):
        codes = [slice(half * 1024 + unit * 512, half * 1024 + unit * 512 + 512) for unit in range(2)]
        for left, right, start in terms:
            at = pl.ds(start, ROWS)
            for unit in range(2):
                load = push(right[at, :], unit)
                pltpu.matmul_acc_lhs(acc_grads[unit], left[codes[unit], at], load)
        for unit in range(2):
            total = pltpu.matmul_pop(acc_grads[unit])
            if first:
                grads[codes[unit], :] = total
            else:
                grads[codes[unit], :] += total

    def grads_weights(chip, half, first=False):
        starts = [aligned(mb * BATCH + chip * 512 + c * ROWS, ROWS) for mb in range(2) for c in range(2)]
        add_grads([(weights, cot, start) for start in starts], half, first)

    def grads_scaled(mb, half):
        add_grads([(scaled, lat, mb * BATCH + c * ROWS) for c in range(4)], half)

    other = (1 - y_lo) * 2 + core
    forward = row_copies(other, fs_sem, fr_sem, partner, partner)
    mate = y_lo * 2 + 1 - core
    other_mate = (1 - y_lo) * 2 + 1 - core

    def ratio_y(mb):
        return [
            remote(part.at[mb], part_y.at[mb, i], ays_sem.at[mb], ayr_sem.at[mb], yc_peer(i))
            for i in range(1, 8)
        ]

    def ratio_xz(mb):
        return [
            remote(part_s.at[mb], part_xz.at[mb, i], axs_sem.at[mb], axr_sem.at[mb], xz_peer(i))
            for i in range(1, 16)
        ]

    ry, rx = [ratio_y(0), ratio_y(1)], [ratio_xz(0), ratio_xz(1)]

    def ratio_first(mb):
        for c in ry[mb]:
            c.start()

    def ratio_second(mb):
        for sem in (ays_sem, ayr_sem):
            wait_bytes(part_y.at[mb, pl.ds(1, 7)], sem.at[mb])
        part_s[mb] = part[mb] + jnp.sum(part_y[mb, 1:8], axis=0)
        for c in rx[mb]:
            c.start()

    def ratio_end(mb):
        for sem in (axs_sem, axr_sem):
            wait_bytes(part_xz.at[mb, pl.ds(1, 15)], sem.at[mb])
        ratio[mb] = part_s[mb] + jnp.sum(part_xz[mb, 1:16], axis=0)

    pass_one([(0, dp), (1, dp)])
    hear_wait(1, "core")
    hear_send(2, "x")
    wait_rows(cr_sem, 0)
    wait_rows(cr_sem, 1)
    pass_one([(0, mate), (1, mate)])
    hear_wait(2, "x")
    hear_send(3, "x")
    wait_rows(gr_sem, 0)
    start_rows(forward, 0)
    pass_one([(0, other)])
    hear_wait(3, "x")
    hear_send(4, "z")
    wait_rows(fr_sem, 0)
    pass_one([(0, other_mate)])
    ratio_first(0)
    hear_wait(4, "z")
    hear_send(5, "z")
    wait_rows(gr_sem, 1)
    start_rows(forward, 1)
    pass_one([(1, other)])
    wait_rows(fr_sem, 1)
    pass_one([(1, other_mate)])
    ratio_first(1)
    hear_wait(5, "z")
    ratio_second(0)
    grads_weights(y_lo, 0, True)
    grads_weights(y_lo, 1, True)
    ratio_second(1)
    grads_weights(1 - y_lo, 0)
    grads_weights(1 - y_lo, 1)

    def second_pass(mb, half):
        r = [
            jnp.concatenate([ratio[mb, 2 * u : 2 * u + 1, :], ratio[mb, 2 * u + 1 : 2 * u + 2, :]], axis=1)
            for u in (2 * half, 2 * half + 1)
        ]
        step = 256
        for k in range(0, CODES, step):
            left = tab_t[:, k : k + step]
            total = None
            for u in range(2):
                start = mb * BATCH + (2 * half + u) * ROWS
                at = slice(start, start + ROWS)
                s = weights[k : k + step, at].astype(F32) * (dots[k : k + step, at] - r[u])
                s_half = s.astype(BF16)
                scaled[k : k + step, at] = s_half
                pair = s[:, :128] + s[:, 128:]
                total = pair if total is None else total + pair
                load = push(s_half, u)
                pltpu.matmul_acc_lhs(acc_work[u][0], left, load)
            if mb == 0 and half == 0:
                col_sum[k : k + step, :] = total
            else:
                col_sum[k : k + step, :] += total
        for u in range(2):
            lg_part[mb, 2 * half + u] = pltpu.matmul_pop(acc_work[u][0]).astype(BF16)

    l_core = [
        [
            remote(
                lg_part.at[mb, h * 2 + 1 - core], lg_core.at[mb, h], lcs_sem.at[mb, h], lcr_sem.at[mb, h], partner
            )
            for h in range(2)
        ]
        for mb in range(2)
    ]

    def place_of(no, hi):
        return (
            pl.ds(aligned(hi * 128 + (no // 2) * 16, 16), 16),
            pl.ds(aligned((no % 2) * 128, 128), 128),
        )

    own_slot = x * 16 + y * 4 + z

    def l_sum_copy(mb, h, i):
        to_x, to_hi, to_z = (x + i // 8) % 4, (y_hi + (i // 4) % 2) % 2, (z + i) % 4
        rows, cols = place_of(to_x * 4 + to_z, to_hi)
        return remote(
            lg_pair.at[mb, h, rows, cols],
            lg_sum.at[mb, own_slot],
            lxs_sem.at[mb],
            lxr_sem.at[mb],
            device(to_x, to_hi * 2 + 1 - h, to_z, core),
        )

    def final_place(mb):
        rows, cols = place_of(part_no, y_hi)
        return lg_all.at[mb, rows, cols]

    def l_all_copy(mb, i):
        to = device(x + i // 8, ((y_hi + i // 4) % 2) * 2 + 1 - y_lo, z + i, core)
        return remote(lg_final.at[mb], final_place(mb), lgs_sem.at[mb], lgr_sem.at[mb], to)

    l_sum = [[[l_sum_copy(mb, h, i) for i in range(32)] for h in range(2)] for mb in range(2)]
    l_all = [[l_all_copy(mb, i) for i in range(32)] for mb in range(2)]

    def latent_0(mb, h):
        l_core[mb][h].start()

    def latent_1(mb, h):
        for sem in (lcs_sem, lcr_sem):
            wait_bytes(lg_core.at[mb, h], sem.at[mb, h])
        lg_pair[mb, h] = (lg_part[mb, h * 2 + core].astype(F32) + lg_core[mb, h].astype(F32)).astype(BF16)
        for c in l_sum[mb][h][1:]:
            c.start()

        @pl.when(y_lo == h)
        def _():
            l_sum[mb][h][0].start()

        @pl.when(y_lo != h)
        def _():
            rows, cols = place_of(part_no, y_hi)
            lg_sum[mb, own_slot] = lg_pair[mb, h, rows, cols]

    def latent_2(mb):
        for sem in (lxs_sem, lxr_sem):
            wait_bytes(lg_sum.at[mb, pl.ds(0, 63)], sem.at[mb])
        total = jnp.sum(lg_sum[mb].astype(F32), axis=0).astype(BF16)
        lg_final[mb] = total
        for c in l_all[mb]:
            c.start()

    def latent_3(mb):
        for sem in (lgs_sem, lgr_sem):
            wait_bytes(lg_sum.at[mb, pl.ds(0, 32)], sem.at[mb])
        lg_out[mb] = lg_all[mb].T

    def adam(i, _):
        at = pl.ds(aligned(i * 256, 256), 256)
        t = tab[at, :].astype(F32)
        sums = jnp.sum(col_sum[at, :], axis=1, keepdims=True)
        grad = grads[at, :] - sums * t
        new_first = first_decay * first_out[at, :] + (1.0 - first_decay) * grad
        new_second = second_decay * second_out[at, :] + (1.0 - second_decay) * grad * grad
        first_hat = new_first * (1.0 / (1.0 - first_decay**ADAM_STEPS))
        second_hat = new_second * (1.0 / (1.0 - second_decay**ADAM_STEPS))
        code_out[at, :] = code_out[at, :] - step_rate * first_hat / (jnp.sqrt(second_hat) + epsilon)
        first_out[at, :] = new_first
        second_out[at, :] = new_second
        return 0

    ratio_end(0)
    second_pass(0, 0)
    latent_0(0, 0)
    second_pass(0, 1)
    latent_0(0, 1)
    latent_1(0, 0)
    ratio_end(1)
    second_pass(1, 0)
    latent_0(1, 0)
    latent_1(0, 1)
    second_pass(1, 1)
    latent_0(1, 1)
    latent_1(1, 0)
    grads_scaled(0, 0)
    latent_1(1, 1)
    grads_scaled(0, 1)
    grads_scaled(1, 0)
    grads_scaled(1, 1)
    mom1_copy.wait()
    mom2_copy.wait()
    lax.fori_loop(0, 3, adam, 0)
    latent_2(0)
    latent_2(1)
    lax.fori_loop(3, 8, adam, 0)
    latent_3(0)
    latent_3(1)
    for sems in (cs_sem, gs_sem, fs_sem):
        wait_rows(sems, 0)
        wait_rows(sems, 1)


def with_sums(*refs):
    def run(g0, g1, w00, w01, w10, w11):
        kernel((g0, g1), ((w00, w01), (w10, w11)), *refs)

    sums = lambda unit, rows: pltpu.ACC(unit)((rows, WIDTH), F32)
    pl.run_scoped(run, sums(0, 512), sums(1, 512), *[sums(unit, 256) for unit in (0, 0, 1, 1)])


def write_out(*refs):
    copies = [pltpu.make_async_copy(refs[i], refs[i + 4], refs[8].at[i]) for i in range(4)]
    for c in copies:
        c.start()
    for c in copies:
        c.wait()


def body(*arrays):
    dma = pltpu.SemaphoreType.DMA
    any_spec, vmem_spec = pl.BlockSpec(memory_space=pl.ANY), pl.BlockSpec(memory_space=pltpu.VMEM)
    code_shape, rows_shape = (CODES, WIDTH), (2, ROWS, WIDTH)
    parts = pl.pallas_call(
        with_sums,
        name="soft_codebook",
        out_shape=(pltpu.VMEM(rows_shape, BF16),) + (pltpu.VMEM(code_shape, F32),) * 3,
        in_specs=[pl.BlockSpec(memory_space=pltpu.HBM)] * 6,
        out_specs=[vmem_spec] * 4,
        scratch_shapes=[
            pltpu.VMEM((ALL, WIDTH), BF16),
            pltpu.VMEM((ALL, WIDTH), BF16),
            pltpu.VMEM((4, 2, ROWS), F32),
            pltpu.VMEM((CODES, WIDTH), BF16),
            pltpu.VMEM((WIDTH, CODES), BF16),
            pltpu.VMEM((CODES, 128), F32),
            pltpu.VMEM((CODES, ALL), BF16),
            pltpu.VMEM((CODES, ALL), BF16),
            pltpu.VMEM((CODES, ALL), F32),
            pltpu.VMEM((CODES, WIDTH), F32),
            pltpu.VMEM((CODES, 128), F32),
            pltpu.VMEM((2, 8, 128), F32),
            pltpu.VMEM((2, 8, 8, 128), F32),
            pltpu.VMEM((2, 8, 128), F32),
            pltpu.VMEM((2, 16, 8, 128), F32),
            pltpu.VMEM((2, 8, 128), F32),
            pltpu.VMEM((2, 4, WIDTH, ROWS), BF16),
            pltpu.VMEM((2, 2, WIDTH, ROWS), BF16),
            pltpu.VMEM((2, 2, WIDTH, ROWS), BF16),
            pltpu.VMEM((2, 64, 16, 128), BF16),
            pltpu.VMEM((2, 16, 128), BF16),
            pltpu.VMEM((2, WIDTH, ROWS), BF16),
            pltpu.SemaphoreType.REGULAR((6,)),
            dma((8,)),
            dma((3,)), dma((3,)), dma((3,)), dma((3,)), dma((3,)), dma((3,)),
            dma((2,)), dma((2,)), dma((2,)), dma((2,)),
            dma((2, 2)), dma((2, 2)), dma((2,)), dma((2,)), dma((2,)), dma((2,)),
        ],
        compiler_params=pltpu.CompilerParams(
            collective_id=0, has_side_effects=True, vmem_limit_bytes=47 * 1024 * 1024
        ),
    )(*[pltpu.with_memory_space_constraint(a, pltpu.HBM) for a in arrays])
    code_array = jax.ShapeDtypeStruct(code_shape, F32)
    return pl.pallas_call(
        write_out,
        name="write_out",
        out_shape=(jax.ShapeDtypeStruct(rows_shape, BF16), code_array, code_array, code_array),
        in_specs=[vmem_spec] * 4,
        out_specs=[any_spec] * 4,
        scratch_shapes=[dma((4,))],
        compiler_params=pltpu.CompilerParams(vmem_limit_bytes=8 * 1024 * 1024),
    )(*[pltpu.with_memory_space_constraint(p, pltpu.VMEM) for p in parts])


def solution(mesh):
    rows, codes = P(None, "dp", None), P(("dp", "code"), None)
    def run(*arrays):
        with jax.sharding.use_abstract_mesh(mesh.abstract_mesh):
            return body(*arrays)

    return jax.shard_map(
        run,
        mesh=mesh,
        in_specs=(rows, rows, P(None, "dp"), codes, codes, codes),
        out_specs=(rows, codes, codes, codes),
        check_vma=False,
    )
```

```python
import functools
import math

import jax
import jax.numpy as jnp
from jax import lax
from jax.experimental import pallas as pl
from jax.experimental.pallas import tpu as pltpu
from jax.sharding import PartitionSpec as P

MESH = pl.DeviceIdType.MESH
ADAM_STEPS = 10
sharpness = 0.25
first_decay = 0.5
second_decay = 0.9
step_rate = 0.01
epsilon = 1e-8

LOG2E = math.log2(math.e)
CODES = 2048
WIDTH = 256
ROWS = 256
BATCH = 1024
ALL = 2 * BATCH
F32, BF16 = jnp.float32, jnp.bfloat16


def place():
    dp, code = lax.axis_index("dp"), lax.axis_index("code")
    return code // 8, ((code // 4) % 2) * 2 + dp // 2, code % 4, dp % 2


def device(x, y, z, core):
    x, y, z, core = x % 4, y % 4, z % 4, core % 2
    return ((y % 2) * 2 + core, x * 8 + (y // 2) * 4 + z)


def away(n):
    return min(n % 4, 4 - n % 4)


def far_first(peers, distance):
    return sorted(peers, key=distance, reverse=True)


def aligned(v, n):
    return pl.multiple_of(v, n)


def kernel(
    acc_grads, acc_work,
    lat_in, cot_in, lse_in, code_in, first_in, second_in,
    lg_out, code_out, first_out, second_out,
    lat, cot, lse, tab, tab_t, bias, weights, scaled, dots, grads, col_sum,
    part, part_y, part_s, part_xz, ratio,
    lg_part, lg_core, lg_pair, lg_sum, lg_final, lg_all, hop_sem,
    load_sem, gs_sem, gr_sem, fs_sem, fr_sem, cs_sem, cr_sem,
    ays_sem, ayr_sem, axs_sem, axr_sem,
    lcs_sem, lcr_sem, lxs_sem, lxr_sem, lgs_sem, lgr_sem,
):
    x, y, z, core = place()
    y_lo, y_hi = y % 2, y // 2
    dp = y_lo * 2 + core
    part_no = x * 4 + z
    partner = device(x, y, z, core + 1)

    barrier = pltpu.get_barrier_semaphore()
    along = {
        "core": [partner],
        "x": [device(x + 1, y, z, core), device(x + 3, y, z, core)],
        "y": [device(x, y + 1, z, core), device(x, y + 3, z, core)],
        "z": [device(x, y, z + 1, core), device(x, y, z + 3, core)],
    }
    for peers in along.values():
        for to in peers:
            pl.semaphore_signal(barrier, inc=1, device_id=to, device_id_type=MESH)

    def hear_send(no, axis):
        for to in along[axis]:
            pl.semaphore_signal(hop_sem.at[no], inc=1, device_id=to, device_id_type=MESH)

    def hear_wait(no, axis):
        pl.semaphore_wait(hop_sem.at[no], len(along[axis]))

    def yc_peer(i):
        return device(x, y + i // 2, z, core + i)

    def xz_peer(i):
        return device(x + i // 4, y, z + i, core)

    def code_peer(i):
        return device(x + i // 4, y + (i // 16) * 2, z + i, core)

    book_copy = pltpu.make_async_copy(code_in, code_out, load_sem.at[0])
    mom1_copy = pltpu.make_async_copy(first_in, first_out, load_sem.at[1])
    mom2_copy = pltpu.make_async_copy(second_in, second_out, load_sem.at[2])

    def rows_of(mb, owner):
        return pl.ds(aligned(mb * BATCH + owner * ROWS, ROWS), ROWS)

    own_copies = []
    for mb in range(2):
        own_copies += [
            pltpu.make_async_copy(lat_in.at[mb], lat.at[rows_of(mb, dp)], load_sem.at[3 + mb]),
            pltpu.make_async_copy(cot_in.at[mb], cot.at[rows_of(mb, dp)], load_sem.at[5 + mb]),
        ]
    own_copies.append(pltpu.make_async_copy(lse_in, lse.at[dp], load_sem.at[7]))
    for c in own_copies:
        c.start()
    book_copy.start()

    def remote(src, dst, send, recv, to):
        return pltpu.make_async_remote_copy(
            src_ref=src, dst_ref=dst, send_sem=send, recv_sem=recv, device_id=to, device_id_type=MESH
        )

    def wait_bytes(ref, sem):
        pltpu.make_async_copy(ref, ref, sem).wait()

    def row_copies(owner, sends, recvs, to_lat, to_cot):
        copies = [[], []]
        for mb in range(2):
            at = rows_of(mb, owner)
            for ref, to in ((lat, to_lat), (cot, to_cot)):
                copies[mb].append(remote(ref.at[at], ref.at[at], sends.at[mb], recvs.at[mb], to))
        copies[0].append(remote(lse.at[owner], lse.at[owner], sends.at[2], recvs.at[2], to_lat))
        return copies

    def start_rows(copies, mb):
        for c in copies[mb]:
            c.start()

    def wait_rows(sems, mb):
        wait_bytes(lat.at[pl.ds(0, 2 * ROWS)], sems.at[mb])
        if mb == 0:
            wait_bytes(lse.at[0], sems.at[2])

    to_partner = row_copies(dp, cs_sem, cr_sem, partner, partner)
    to_y = row_copies(dp, gs_sem, gr_sem, device(x, y + 1, z, core), device(x, y + 3, z, core))
    pl.semaphore_wait(barrier, 7)
    for c in own_copies:
        c.wait()
    start_rows(to_y, 0)
    hear_send(0, "y")
    start_rows(to_partner, 0)
    start_rows(to_partner, 1)

    book_copy.wait()

    def make_table(i, _):
        at = pl.ds(aligned(i * 256, 256), 256)
        t = code_out[at, :].astype(BF16)
        tab[at, :] = t
        wide = t.astype(F32)
        tab_t[:, at] = t.T
        squares = jnp.sum(wide * wide, axis=1, keepdims=True) * (0.5 * sharpness * LOG2E)
        bias[at, :] = jnp.broadcast_to(squares, (256, 128))
        return 0

    lax.fori_loop(0, CODES // 256, make_table, 0)
    start_rows(to_y, 1)
    mom1_copy.start()
    mom2_copy.start()
    hear_wait(0, "y")
    hear_send(1, "core")

    staged = [0, 0]

    def push(rhs, unit, transpose=False):
        staged[unit] = 1 - staged[unit]
        pltpu.matmul_push_rhs(rhs, staged[unit], unit, transpose=transpose)
        return staged[unit]

    def pass_one(pairs):
        places = [rows_of(mb, owner) for mb, owner in pairs]
        shifts = [lse[owner, mb : mb + 1, :] * LOG2E for mb, owner in pairs]
        totals = [jnp.zeros((8, ROWS), F32) for _ in pairs]
        step = 256
        tiles = [(i, k) for i in range(len(pairs)) for k in range(0, CODES, step)]

        def multiply(n):
            i, k = tiles[n]
            for unit, rows in enumerate((lat, cot)):
                load = push(rows[places[i], :], unit, transpose=True) if k == 0 else None
                pltpu.matmul_acc_lhs(acc_work[unit][n % 2], tab[k : k + step, :], load)

        multiply(0)
        for n, (i, k) in enumerate(tiles):
            if n + 1 < len(tiles):
                multiply(n + 1)
            b = bias[k : k + step, :]
            logits = pltpu.matmul_pop(acc_work[0][n % 2])
            inner = pltpu.matmul_pop(acc_work[1][n % 2]) * sharpness
            w = jnp.exp2(logits * (sharpness * LOG2E) - jnp.concatenate([b, b], axis=1) - shifts[i])
            totals[i] = totals[i] + jnp.sum((w * inner).reshape(step // 8, 8, ROWS), axis=0)
            weights[k : k + step, places[i]] = w.astype(BF16)
            dots[k : k + step, places[i]] = inner
        for (mb, owner), total in zip(pairs, totals):
            row = jnp.sum(total, axis=0, keepdims=True)
            part[mb, pl.ds(owner * 2, 1), :] = row[:, :128]
            part[mb, pl.ds(owner * 2 + 1, 1), :] = row[:, 128:]

    def add_grads(terms, half, first=False):
        codes = [slice(half * 1024 + unit * 512, half * 1024 + unit * 512 + 512) for unit in range(2)]
        for left, right, start in terms:
            at = pl.ds(start, ROWS)
            for unit in range(2):
                load = push(right[at, :], unit)
                pltpu.matmul_acc_lhs(acc_grads[unit], left[codes[unit], at], load)
        for unit in range(2):
            total = pltpu.matmul_pop(acc_grads[unit])
            if first:
                grads[codes[unit], :] = total
            else:
                grads[codes[unit], :] += total

    def grads_weights(chip, half, first=False):
        starts = [aligned(mb * BATCH + chip * 512 + c * ROWS, ROWS) for mb in range(2) for c in range(2)]
        add_grads([(weights, cot, start) for start in starts], half, first)

    def grads_scaled(mb, half):
        add_grads([(scaled, lat, mb * BATCH + c * ROWS) for c in range(4)], half)

    other = (1 - y_lo) * 2 + core
    forward = row_copies(other, fs_sem, fr_sem, partner, partner)
    mate = y_lo * 2 + 1 - core
    other_mate = (1 - y_lo) * 2 + 1 - core

    def ratio_y(mb):
        return [
            remote(part.at[mb], part_y.at[mb, i], ays_sem.at[mb], ayr_sem.at[mb], yc_peer(i))
            for i in far_first(range(1, 8), lambda i: away(i // 2) + i % 2)
        ]

    def ratio_xz(mb):
        return [
            remote(part_s.at[mb], part_xz.at[mb, i], axs_sem.at[mb], axr_sem.at[mb], xz_peer(i))
            for i in far_first(range(1, 16), lambda i: away(i // 4) + away(i))
        ]

    ry, rx = [ratio_y(0), ratio_y(1)], [ratio_xz(0), ratio_xz(1)]

    def ratio_first(mb):
        for c in ry[mb]:
            c.start()

    def ratio_second(mb):
        for sem in (ays_sem, ayr_sem):
            wait_bytes(part_y.at[mb, pl.ds(1, 7)], sem.at[mb])
        part_s[mb] = part[mb] + jnp.sum(part_y[mb, 1:8], axis=0)
        for c in rx[mb]:
            c.start()

    def ratio_end(mb):
        for sem in (axs_sem, axr_sem):
            wait_bytes(part_xz.at[mb, pl.ds(1, 15)], sem.at[mb])
        ratio[mb] = part_s[mb] + jnp.sum(part_xz[mb, 1:16], axis=0)

    pass_one([(0, dp), (1, dp)])
    hear_wait(1, "core")
    hear_send(2, "x")
    wait_rows(cr_sem, 0)
    wait_rows(cr_sem, 1)
    pass_one([(0, mate), (1, mate)])
    hear_wait(2, "x")
    hear_send(3, "x")
    wait_rows(gr_sem, 0)
    start_rows(forward, 0)
    pass_one([(0, other)])
    hear_wait(3, "x")
    hear_send(4, "z")
    wait_rows(fr_sem, 0)
    pass_one([(0, other_mate)])
    ratio_first(0)
    hear_wait(4, "z")
    hear_send(5, "z")
    wait_rows(gr_sem, 1)
    start_rows(forward, 1)
    pass_one([(1, other)])
    wait_rows(fr_sem, 1)
    pass_one([(1, other_mate)])
    ratio_first(1)
    hear_wait(5, "z")
    ratio_second(0)
    grads_weights(y_lo, 0, True)
    grads_weights(y_lo, 1, True)
    ratio_second(1)
    grads_weights(1 - y_lo, 0)
    grads_weights(1 - y_lo, 1)

    def second_pass(mb, half):
        r = [
            jnp.concatenate([ratio[mb, 2 * u : 2 * u + 1, :], ratio[mb, 2 * u + 1 : 2 * u + 2, :]], axis=1)
            for u in (2 * half, 2 * half + 1)
        ]
        step = 256
        for k in range(0, CODES, step):
            left = tab_t[:, k : k + step]
            total = None
            for u in range(2):
                start = mb * BATCH + (2 * half + u) * ROWS
                at = slice(start, start + ROWS)
                s = weights[k : k + step, at].astype(F32) * (dots[k : k + step, at] - r[u])
                s_half = s.astype(BF16)
                scaled[k : k + step, at] = s_half
                pair = s[:, :128] + s[:, 128:]
                total = pair if total is None else total + pair
                load = push(s_half, u)
                pltpu.matmul_acc_lhs(acc_work[u][0], left, load)
            if mb == 0 and half == 0:
                col_sum[k : k + step, :] = total
            else:
                col_sum[k : k + step, :] += total
        for u in range(2):
            lg_part[mb, 2 * half + u] = pltpu.matmul_pop(acc_work[u][0]).astype(BF16)

    l_core = [
        [
            remote(
                lg_part.at[mb, h * 2 + 1 - core], lg_core.at[mb, h], lcs_sem.at[mb, h], lcr_sem.at[mb, h], partner
            )
            for h in range(2)
        ]
        for mb in range(2)
    ]

    def place_of(no, hi):
        return (
            pl.ds(aligned(hi * 128 + (no // 2) * 16, 16), 16),
            pl.ds(aligned((no % 2) * 128, 128), 128),
        )

    own_slot = x * 16 + y * 4 + z

    def l_sum_copy(mb, h, i):
        to_x, to_hi, to_z = (x + i // 8) % 4, (y_hi + (i // 4) % 2) % 2, (z + i) % 4
        rows, cols = place_of(to_x * 4 + to_z, to_hi)
        return remote(
            lg_pair.at[mb, h, rows, cols],
            lg_sum.at[mb, own_slot],
            lxs_sem.at[mb],
            lxr_sem.at[mb],
            device(to_x, to_hi * 2 + 1 - h, to_z, core),
        )

    def final_place(mb):
        rows, cols = place_of(part_no, y_hi)
        return lg_all.at[mb, rows, cols]

    def l_all_copy(mb, i):
        to = device(x + i // 8, ((y_hi + i // 4) % 2) * 2 + 1 - y_lo, z + i, core)
        return remote(lg_final.at[mb], final_place(mb), lgs_sem.at[mb], lgr_sem.at[mb], to)

    l_sum = [[[l_sum_copy(mb, h, i) for i in range(32)] for h in range(2)] for mb in range(2)]
    l_all = [
        [l_all_copy(mb, i) for i in far_first(range(32), lambda i: away(i // 8) + away(i))] for mb in range(2)
    ]

    def latent_0(mb, h):
        l_core[mb][h].start()

    def latent_1(mb, h):
        for sem in (lcs_sem, lcr_sem):
            wait_bytes(lg_core.at[mb, h], sem.at[mb, h])
        lg_pair[mb, h] = (lg_part[mb, h * 2 + core].astype(F32) + lg_core[mb, h].astype(F32)).astype(BF16)
        for i in far_first(range(1, 32), lambda i: away(i // 8) + away(i) + (i // 4) % 2):
            l_sum[mb][h][i].start()

        @pl.when(y_lo == h)
        def _():
            l_sum[mb][h][0].start()

        @pl.when(y_lo != h)
        def _():
            rows, cols = place_of(part_no, y_hi)
            lg_sum[mb, own_slot] = lg_pair[mb, h, rows, cols]

    def latent_2(mb):
        for sem in (lxs_sem, lxr_sem):
            wait_bytes(lg_sum.at[mb, pl.ds(0, 63)], sem.at[mb])
        total = jnp.sum(lg_sum[mb].astype(F32), axis=0).astype(BF16)
        lg_final[mb] = total
        for c in l_all[mb]:
            c.start()

    def latent_3(mb):
        for sem in (lgs_sem, lgr_sem):
            wait_bytes(lg_sum.at[mb, pl.ds(0, 32)], sem.at[mb])
        lg_out[mb] = lg_all[mb].T

    def adam(i, _):
        at = pl.ds(aligned(i * 256, 256), 256)
        t = tab[at, :].astype(F32)
        sums = jnp.sum(col_sum[at, :], axis=1, keepdims=True)
        grad = grads[at, :] - sums * t
        new_first = first_decay * first_out[at, :] + (1.0 - first_decay) * grad
        new_second = second_decay * second_out[at, :] + (1.0 - second_decay) * grad * grad
        first_hat = new_first * (1.0 / (1.0 - first_decay**ADAM_STEPS))
        second_hat = new_second * (1.0 / (1.0 - second_decay**ADAM_STEPS))
        code_out[at, :] = code_out[at, :] - step_rate * first_hat / (jnp.sqrt(second_hat) + epsilon)
        first_out[at, :] = new_first
        second_out[at, :] = new_second
        return 0

    ratio_end(0)
    second_pass(0, 0)
    latent_0(0, 0)
    second_pass(0, 1)
    latent_0(0, 1)
    latent_1(0, 0)
    ratio_end(1)
    second_pass(1, 0)
    latent_0(1, 0)
    latent_1(0, 1)
    second_pass(1, 1)
    latent_0(1, 1)
    latent_1(1, 0)
    grads_scaled(0, 0)
    latent_1(1, 1)
    grads_scaled(0, 1)
    grads_scaled(1, 0)
    grads_scaled(1, 1)
    mom1_copy.wait()
    mom2_copy.wait()
    lax.fori_loop(0, 3, adam, 0)
    latent_2(0)
    latent_2(1)
    lax.fori_loop(3, 8, adam, 0)
    latent_3(0)
    latent_3(1)
    for sems in (cs_sem, gs_sem, fs_sem):
        wait_rows(sems, 0)
        wait_rows(sems, 1)


def with_sums(*refs):
    def run(g0, g1, w00, w01, w10, w11):
        kernel((g0, g1), ((w00, w01), (w10, w11)), *refs)

    sums = lambda unit, rows: pltpu.ACC(unit)((rows, WIDTH), F32)
    pl.run_scoped(run, sums(0, 512), sums(1, 512), *[sums(unit, 256) for unit in (0, 0, 1, 1)])


def write_out(*refs):
    copies = [pltpu.make_async_copy(refs[i], refs[i + 4], refs[8].at[i]) for i in range(4)]
    for c in copies:
        c.start()
    for c in copies:
        c.wait()


def body(*arrays):
    dma = pltpu.SemaphoreType.DMA
    any_spec, vmem_spec = pl.BlockSpec(memory_space=pl.ANY), pl.BlockSpec(memory_space=pltpu.VMEM)
    code_shape, rows_shape = (CODES, WIDTH), (2, ROWS, WIDTH)
    parts = pl.pallas_call(
        with_sums,
        name="soft_codebook",
        out_shape=(pltpu.VMEM(rows_shape, BF16),) + (pltpu.VMEM(code_shape, F32),) * 3,
        in_specs=[pl.BlockSpec(memory_space=pltpu.HBM)] * 6,
        out_specs=[vmem_spec] * 4,
        scratch_shapes=[
            pltpu.VMEM((ALL, WIDTH), BF16),
            pltpu.VMEM((ALL, WIDTH), BF16),
            pltpu.VMEM((4, 2, ROWS), F32),
            pltpu.VMEM((CODES, WIDTH), BF16),
            pltpu.VMEM((WIDTH, CODES), BF16),
            pltpu.VMEM((CODES, 128), F32),
            pltpu.VMEM((CODES, ALL), BF16),
            pltpu.VMEM((CODES, ALL), BF16),
            pltpu.VMEM((CODES, ALL), F32),
            pltpu.VMEM((CODES, WIDTH), F32),
            pltpu.VMEM((CODES, 128), F32),
            pltpu.VMEM((2, 8, 128), F32),
            pltpu.VMEM((2, 8, 8, 128), F32),
            pltpu.VMEM((2, 8, 128), F32),
            pltpu.VMEM((2, 16, 8, 128), F32),
            pltpu.VMEM((2, 8, 128), F32),
            pltpu.VMEM((2, 4, WIDTH, ROWS), BF16),
            pltpu.VMEM((2, 2, WIDTH, ROWS), BF16),
            pltpu.VMEM((2, 2, WIDTH, ROWS), BF16),
            pltpu.VMEM((2, 64, 16, 128), BF16),
            pltpu.VMEM((2, 16, 128), BF16),
            pltpu.VMEM((2, WIDTH, ROWS), BF16),
            pltpu.SemaphoreType.REGULAR((6,)),
            dma((8,)),
            dma((3,)), dma((3,)), dma((3,)), dma((3,)), dma((3,)), dma((3,)),
            dma((2,)), dma((2,)), dma((2,)), dma((2,)),
            dma((2, 2)), dma((2, 2)), dma((2,)), dma((2,)), dma((2,)), dma((2,)),
        ],
        compiler_params=pltpu.CompilerParams(
            collective_id=0, has_side_effects=True, vmem_limit_bytes=47 * 1024 * 1024
        ),
    )(*[pltpu.with_memory_space_constraint(a, pltpu.HBM) for a in arrays])
    code_array = jax.ShapeDtypeStruct(code_shape, F32)
    return pl.pallas_call(
        write_out,
        name="write_out",
        out_shape=(jax.ShapeDtypeStruct(rows_shape, BF16), code_array, code_array, code_array),
        in_specs=[vmem_spec] * 4,
        out_specs=[any_spec] * 4,
        scratch_shapes=[dma((4,))],
        compiler_params=pltpu.CompilerParams(vmem_limit_bytes=8 * 1024 * 1024),
    )(*[pltpu.with_memory_space_constraint(p, pltpu.VMEM) for p in parts])


def solution(mesh):
    rows, codes = P(None, "dp", None), P(("dp", "code"), None)
    def run(*arrays):
        with jax.sharding.use_abstract_mesh(mesh.abstract_mesh):
            return body(*arrays)

    return jax.shard_map(
        run,
        mesh=mesh,
        in_specs=(rows, rows, P(None, "dp"), codes, codes, codes),
        out_specs=(rows, codes, codes, codes),
        check_vma=False,
    )
```

```python
import functools
import math

import jax
import jax.numpy as jnp
from jax import lax
from jax.experimental import pallas as pl
from jax.experimental.pallas import tpu as pltpu
from jax.sharding import PartitionSpec as P

MESH = pl.DeviceIdType.MESH
ADAM_STEPS = 10
sharpness = 0.25
first_decay = 0.5
second_decay = 0.9
step_rate = 0.01
epsilon = 1e-8

LOG2E = math.log2(math.e)
CODES = 2048
WIDTH = 256
ROWS = 256
BATCH = 1024
ALL = 2 * BATCH
F32, BF16 = jnp.float32, jnp.bfloat16


def place():
    dp, code = lax.axis_index("dp"), lax.axis_index("code")
    return code // 8, ((code // 4) % 2) * 2 + dp // 2, code % 4, dp % 2


def device(x, y, z, core):
    x, y, z, core = x % 4, y % 4, z % 4, core % 2
    return ((y % 2) * 2 + core, x * 8 + (y // 2) * 4 + z)


def away(n):
    return min(n % 4, 4 - n % 4)


def far_first(peers, distance):
    return sorted(peers, key=distance, reverse=True)


def aligned(v, n):
    return pl.multiple_of(v, n)


def kernel(
    acc_grads, acc_work,
    lat_in, cot_in, lse_in, code_in, first_in, second_in,
    lg_out, code_out, first_out, second_out,
    lat, cot, lse, tab, tab_t, bias, weights, scaled, dots, grads, col_sum,
    part, part_y, part_s, part_xz, ratio,
    lg_part, lg_core, lg_pair, lg_sum, lg_final, lg_all, hop_sem,
    load_sem, gs_sem, gr_sem, fs_sem, fr_sem, cs_sem, cr_sem,
    ays_sem, ayr_sem, axs_sem, axr_sem,
    lcs_sem, lcr_sem, lxs_sem, lxr_sem, lgs_sem, lgr_sem,
):
    x, y, z, core = place()
    y_lo, y_hi = y % 2, y // 2
    dp = y_lo * 2 + core
    part_no = x * 4 + z
    partner = device(x, y, z, core + 1)

    barrier = pltpu.get_barrier_semaphore()
    along = {
        "core": [partner],
        "x": [device(x + 1, y, z, core), device(x + 3, y, z, core)],
        "y": [device(x, y + 1, z, core), device(x, y + 3, z, core)],
        "z": [device(x, y, z + 1, core), device(x, y, z + 3, core)],
    }
    for peers in along.values():
        for to in peers:
            pl.semaphore_signal(barrier, inc=1, device_id=to, device_id_type=MESH)

    def hear_send(no, axis):
        for to in along[axis]:
            pl.semaphore_signal(hop_sem.at[no], inc=1, device_id=to, device_id_type=MESH)

    def hear_wait(no, axis):
        pl.semaphore_wait(hop_sem.at[no], len(along[axis]))

    def yc_peer(i):
        return device(x, y + i // 2, z, core + i)

    def xz_peer(i):
        return device(x + i // 4, y, z + i, core)

    def code_peer(i):
        return device(x + i // 4, y + (i // 16) * 2, z + i, core)

    book_copy = pltpu.make_async_copy(code_in, code_out, load_sem.at[0])
    mom1_copy = pltpu.make_async_copy(first_in, first_out, load_sem.at[1])
    mom2_copy = pltpu.make_async_copy(second_in, second_out, load_sem.at[2])

    def rows_of(mb, owner):
        return pl.ds(aligned(mb * BATCH + owner * ROWS, ROWS), ROWS)

    own_copies = []
    for mb in range(2):
        own_copies += [
            pltpu.make_async_copy(lat_in.at[mb], lat.at[rows_of(mb, dp)], load_sem.at[3 + mb]),
            pltpu.make_async_copy(cot_in.at[mb], cot.at[rows_of(mb, dp)], load_sem.at[5 + mb]),
        ]
    own_copies.append(pltpu.make_async_copy(lse_in, lse.at[dp], load_sem.at[7]))
    for c in own_copies:
        c.start()
    book_copy.start()

    def remote(src, dst, send, recv, to):
        return pltpu.make_async_remote_copy(
            src_ref=src, dst_ref=dst, send_sem=send, recv_sem=recv, device_id=to, device_id_type=MESH
        )

    def wait_bytes(ref, sem):
        pltpu.make_async_copy(ref, ref, sem).wait()

    def row_copies(owner, sends, recvs, to_lat, to_cot):
        copies = [[], []]
        for mb in range(2):
            at = rows_of(mb, owner)
            for ref, to in ((lat, to_lat), (cot, to_cot)):
                copies[mb].append(remote(ref.at[at], ref.at[at], sends.at[mb], recvs.at[mb], to))
        copies[0].append(remote(lse.at[owner], lse.at[owner], sends.at[2], recvs.at[2], to_lat))
        return copies

    def start_rows(copies, mb):
        for c in copies[mb]:
            c.start()

    def wait_rows(sems, mb):
        wait_bytes(lat.at[pl.ds(0, 2 * ROWS)], sems.at[mb])
        if mb == 0:
            wait_bytes(lse.at[0], sems.at[2])

    to_partner = row_copies(dp, cs_sem, cr_sem, partner, partner)
    to_y = row_copies(dp, gs_sem, gr_sem, device(x, y + 1, z, core), device(x, y + 3, z, core))
    pl.semaphore_wait(barrier, 7)
    for c in own_copies:
        c.wait()
    start_rows(to_y, 0)
    hear_send(0, "y")
    start_rows(to_partner, 0)

    book_copy.wait()

    def make_table(i, _):
        at = pl.ds(aligned(i * 256, 256), 256)
        t = code_out[at, :].astype(BF16)
        tab[at, :] = t
        wide = t.astype(F32)
        tab_t[:, at] = t.T
        squares = jnp.sum(wide * wide, axis=1, keepdims=True) * (0.5 * sharpness * LOG2E)
        bias[at, :] = jnp.broadcast_to(squares, (256, 128))
        return 0

    lax.fori_loop(0, CODES // 256, make_table, 0)
    start_rows(to_partner, 1)
    start_rows(to_y, 1)
    mom1_copy.start()
    mom2_copy.start()
    hear_wait(0, "y")
    hear_send(1, "core")

    staged = [0, 0]

    def push(rhs, unit, transpose=False):
        staged[unit] = 1 - staged[unit]
        pltpu.matmul_push_rhs(rhs, staged[unit], unit, transpose=transpose)
        return staged[unit]

    def pass_one(pairs):
        places = [rows_of(mb, owner) for mb, owner in pairs]
        shifts = [lse[owner, mb : mb + 1, :] * LOG2E for mb, owner in pairs]
        totals = [jnp.zeros((8, ROWS), F32) for _ in pairs]
        step = 256
        tiles = [(i, k) for i in range(len(pairs)) for k in range(0, CODES, step)]

        def multiply(n):
            i, k = tiles[n]
            for unit, rows in enumerate((lat, cot)):
                load = push(rows[places[i], :], unit, transpose=True) if k == 0 else None
                pltpu.matmul_acc_lhs(acc_work[unit][n % 2], tab[k : k + step, :], load)

        multiply(0)
        for n, (i, k) in enumerate(tiles):
            if n + 1 < len(tiles):
                multiply(n + 1)
            b = bias[k : k + step, :]
            logits = pltpu.matmul_pop(acc_work[0][n % 2])
            inner = pltpu.matmul_pop(acc_work[1][n % 2]) * sharpness
            w = jnp.exp2(logits * (sharpness * LOG2E) - jnp.concatenate([b, b], axis=1) - shifts[i])
            totals[i] = totals[i] + jnp.sum((w * inner).reshape(step // 8, 8, ROWS), axis=0)
            weights[k : k + step, places[i]] = w.astype(BF16)
            dots[k : k + step, places[i]] = inner
        for (mb, owner), total in zip(pairs, totals):
            row = jnp.sum(total, axis=0, keepdims=True)
            part[mb, pl.ds(owner * 2, 1), :] = row[:, :128]
            part[mb, pl.ds(owner * 2 + 1, 1), :] = row[:, 128:]

    def add_grads(terms, half, first=False):
        codes = [slice(half * 1024 + unit * 512, half * 1024 + unit * 512 + 512) for unit in range(2)]
        for left, right, start in terms:
            at = pl.ds(start, ROWS)
            for unit in range(2):
                load = push(right[at, :], unit)
                pltpu.matmul_acc_lhs(acc_grads[unit], left[codes[unit], at], load)
        for unit in range(2):
            total = pltpu.matmul_pop(acc_grads[unit])
            if first:
                grads[codes[unit], :] = total
            else:
                grads[codes[unit], :] += total

    def grads_weights(chip, half, first=False):
        starts = [aligned(mb * BATCH + chip * 512 + c * ROWS, ROWS) for mb in range(2) for c in range(2)]
        add_grads([(weights, cot, start) for start in starts], half, first)

    def grads_scaled(mb, half):
        add_grads([(scaled, lat, mb * BATCH + c * ROWS) for c in range(4)], half)
        for k in range(half * 1024, half * 1024 + 1024, 128):
            total = None
            for c in range(mb * BATCH, (mb + 1) * BATCH, 128):
                block = scaled[k : k + 128, c : c + 128].astype(F32)
                total = block if total is None else total + block
            if mb == 0:
                col_sum[k : k + 128, :] = total
            else:
                col_sum[k : k + 128, :] += total

    other = (1 - y_lo) * 2 + core
    forward = row_copies(other, fs_sem, fr_sem, partner, partner)
    mate = y_lo * 2 + 1 - core
    other_mate = (1 - y_lo) * 2 + 1 - core

    def ratio_y(mb):
        return [
            remote(part.at[mb], part_y.at[mb, i], ays_sem.at[mb], ayr_sem.at[mb], yc_peer(i))
            for i in far_first(range(1, 8), lambda i: away(i // 2) + i % 2)
        ]

    def ratio_xz(mb):
        return [
            remote(part_s.at[mb], part_xz.at[mb, i], axs_sem.at[mb], axr_sem.at[mb], xz_peer(i))
            for i in far_first(range(1, 16), lambda i: away(i // 4) + away(i))
        ]

    ry, rx = [ratio_y(0), ratio_y(1)], [ratio_xz(0), ratio_xz(1)]

    def ratio_first(mb):
        for c in ry[mb]:
            c.start()

    def ratio_second(mb):
        for sem in (ays_sem, ayr_sem):
            wait_bytes(part_y.at[mb, pl.ds(1, 7)], sem.at[mb])
        part_s[mb] = part[mb] + jnp.sum(part_y[mb, 1:8], axis=0)
        for c in rx[mb]:
            c.start()

    def ratio_end(mb):
        for sem in (axs_sem, axr_sem):
            wait_bytes(part_xz.at[mb, pl.ds(1, 15)], sem.at[mb])
        ratio[mb] = part_s[mb] + jnp.sum(part_xz[mb, 1:16], axis=0)

    pass_one([(0, dp), (1, dp)])
    hear_wait(1, "core")
    hear_send(2, "x")
    wait_rows(cr_sem, 0)
    wait_rows(cr_sem, 1)
    pass_one([(0, mate), (1, mate)])
    hear_wait(2, "x")
    hear_send(3, "x")
    wait_rows(gr_sem, 0)
    start_rows(forward, 0)
    pass_one([(0, other)])
    hear_wait(3, "x")
    hear_send(4, "z")
    wait_rows(fr_sem, 0)
    pass_one([(0, other_mate)])
    ratio_first(0)
    hear_wait(4, "z")
    hear_send(5, "z")
    wait_rows(gr_sem, 1)
    start_rows(forward, 1)
    pass_one([(1, other)])
    wait_rows(fr_sem, 1)
    pass_one([(1, other_mate)])
    ratio_first(1)
    hear_wait(5, "z")
    ratio_second(0)
    grads_weights(y_lo, 0, True)
    grads_weights(y_lo, 1, True)
    ratio_second(1)
    grads_weights(1 - y_lo, 0)
    grads_weights(1 - y_lo, 1)

    def second_pass(mb, half):
        r = [
            jnp.concatenate([ratio[mb, 2 * u : 2 * u + 1, :], ratio[mb, 2 * u + 1 : 2 * u + 2, :]], axis=1)
            for u in (2 * half, 2 * half + 1)
        ]
        step = 256
        for k in range(0, CODES, step):
            left = tab_t[:, k : k + step]
            for u in range(2):
                start = mb * BATCH + (2 * half + u) * ROWS
                at = slice(start, start + ROWS)
                s = weights[k : k + step, at].astype(F32) * (dots[k : k + step, at] - r[u])
                s_half = s.astype(BF16)
                scaled[k : k + step, at] = s_half
                load = push(s_half, u)
                pltpu.matmul_acc_lhs(acc_work[u][0], left, load)
        for u in range(2):
            lg_part[mb, 2 * half + u] = pltpu.matmul_pop(acc_work[u][0]).astype(BF16)

    l_core = [
        [
            remote(
                lg_part.at[mb, h * 2 + 1 - core], lg_core.at[mb, h], lcs_sem.at[mb, h], lcr_sem.at[mb, h], partner
            )
            for h in range(2)
        ]
        for mb in range(2)
    ]

    def place_of(no, hi):
        return (
            pl.ds(aligned(hi * 128 + (no // 2) * 16, 16), 16),
            pl.ds(aligned((no % 2) * 128, 128), 128),
        )

    own_slot = x * 16 + y * 4 + z

    def l_sum_copy(mb, h, i):
        to_x, to_hi, to_z = (x + i // 8) % 4, (y_hi + (i // 4) % 2) % 2, (z + i) % 4
        rows, cols = place_of(to_x * 4 + to_z, to_hi)
        return remote(
            lg_pair.at[mb, h, rows, cols],
            lg_sum.at[mb, own_slot],
            lxs_sem.at[mb],
            lxr_sem.at[mb],
            device(to_x, to_hi * 2 + 1 - h, to_z, core),
        )

    def final_place(mb):
        rows, cols = place_of(part_no, y_hi)
        return lg_all.at[mb, rows, cols]

    def l_all_copy(mb, i):
        to = device(x + i // 8, ((y_hi + i // 4) % 2) * 2 + 1 - y_lo, z + i, core)
        return remote(lg_final.at[mb], final_place(mb), lgs_sem.at[mb], lgr_sem.at[mb], to)

    l_sum = [[[l_sum_copy(mb, h, i) for i in range(32)] for h in range(2)] for mb in range(2)]
    l_all = [
        [l_all_copy(mb, i) for i in far_first(range(32), lambda i: away(i // 8) + away(i))] for mb in range(2)
    ]

    def latent_0(mb, h):
        l_core[mb][h].start()

    def latent_1(mb, h):
        for sem in (lcs_sem, lcr_sem):
            wait_bytes(lg_core.at[mb, h], sem.at[mb, h])
        lg_pair[mb, h] = (lg_part[mb, h * 2 + core].astype(F32) + lg_core[mb, h].astype(F32)).astype(BF16)
        for i in far_first(range(1, 32), lambda i: away(i // 8) + away(i) + (i // 4) % 2):
            l_sum[mb][h][i].start()

        @pl.when(y_lo == h)
        def _():
            l_sum[mb][h][0].start()

        @pl.when(y_lo != h)
        def _():
            rows, cols = place_of(part_no, y_hi)
            lg_sum[mb, own_slot] = lg_pair[mb, h, rows, cols]

    def latent_2(mb):
        for sem in (lxs_sem, lxr_sem):
            wait_bytes(lg_sum.at[mb, pl.ds(0, 63)], sem.at[mb])
        total = jnp.sum(lg_sum[mb].astype(F32), axis=0).astype(BF16)
        lg_final[mb] = total
        for c in l_all[mb]:
            c.start()

    def latent_3(mb):
        for sem in (lgs_sem, lgr_sem):
            wait_bytes(lg_sum.at[mb, pl.ds(0, 32)], sem.at[mb])
        lg_out[mb] = lg_all[mb].T

    def adam(i, _):
        at = pl.ds(aligned(i * 256, 256), 256)
        t = tab[at, :].astype(F32)
        sums = jnp.sum(col_sum[at, :], axis=1, keepdims=True)
        grad = grads[at, :] - sums * t
        new_first = first_decay * first_out[at, :] + (1.0 - first_decay) * grad
        new_second = second_decay * second_out[at, :] + (1.0 - second_decay) * grad * grad
        first_hat = new_first * (1.0 / (1.0 - first_decay**ADAM_STEPS))
        second_hat = new_second * (1.0 / (1.0 - second_decay**ADAM_STEPS))
        code_out[at, :] = code_out[at, :] - step_rate * first_hat / (jnp.sqrt(second_hat) + epsilon)
        first_out[at, :] = new_first
        second_out[at, :] = new_second
        return 0

    ratio_end(0)
    second_pass(0, 0)
    latent_0(0, 0)
    second_pass(0, 1)
    latent_0(0, 1)
    latent_1(0, 0)
    ratio_end(1)
    second_pass(1, 0)
    latent_0(1, 0)
    latent_1(0, 1)
    second_pass(1, 1)
    latent_0(1, 1)
    latent_1(1, 0)
    grads_scaled(0, 0)
    latent_1(1, 1)
    grads_scaled(0, 1)
    grads_scaled(1, 0)
    grads_scaled(1, 1)
    mom1_copy.wait()
    mom2_copy.wait()
    lax.fori_loop(0, 3, adam, 0)
    latent_2(0)
    latent_2(1)
    lax.fori_loop(3, 8, adam, 0)
    latent_3(0)
    latent_3(1)
    for sems in (cs_sem, gs_sem, fs_sem):
        wait_rows(sems, 0)
        wait_rows(sems, 1)


def with_sums(*refs):
    def run(g0, g1, w00, w01, w10, w11):
        kernel((g0, g1), ((w00, w01), (w10, w11)), *refs)

    sums = lambda unit, rows: pltpu.ACC(unit)((rows, WIDTH), F32)
    pl.run_scoped(run, sums(0, 512), sums(1, 512), *[sums(unit, 256) for unit in (0, 0, 1, 1)])


def write_out(*refs):
    copies = [pltpu.make_async_copy(refs[i], refs[i + 4], refs[8].at[i]) for i in range(4)]
    for c in copies:
        c.start()
    for c in copies:
        c.wait()


def body(*arrays):
    dma = pltpu.SemaphoreType.DMA
    any_spec, vmem_spec = pl.BlockSpec(memory_space=pl.ANY), pl.BlockSpec(memory_space=pltpu.VMEM)
    code_shape, rows_shape = (CODES, WIDTH), (2, ROWS, WIDTH)
    parts = pl.pallas_call(
        with_sums,
        name="soft_codebook",
        out_shape=(pltpu.VMEM(rows_shape, BF16),) + (pltpu.VMEM(code_shape, F32),) * 3,
        in_specs=[pl.BlockSpec(memory_space=pltpu.HBM)] * 6,
        out_specs=[vmem_spec] * 4,
        scratch_shapes=[
            pltpu.VMEM((ALL, WIDTH), BF16),
            pltpu.VMEM((ALL, WIDTH), BF16),
            pltpu.VMEM((4, 2, ROWS), F32),
            pltpu.VMEM((CODES, WIDTH), BF16),
            pltpu.VMEM((WIDTH, CODES), BF16),
            pltpu.VMEM((CODES, 128), F32),
            pltpu.VMEM((CODES, ALL), BF16),
            pltpu.VMEM((CODES, ALL), BF16),
            pltpu.VMEM((CODES, ALL), F32),
            pltpu.VMEM((CODES, WIDTH), F32),
            pltpu.VMEM((CODES, 128), F32),
            pltpu.VMEM((2, 8, 128), F32),
            pltpu.VMEM((2, 8, 8, 128), F32),
            pltpu.VMEM((2, 8, 128), F32),
            pltpu.VMEM((2, 16, 8, 128), F32),
            pltpu.VMEM((2, 8, 128), F32),
            pltpu.VMEM((2, 4, WIDTH, ROWS), BF16),
            pltpu.VMEM((2, 2, WIDTH, ROWS), BF16),
            pltpu.VMEM((2, 2, WIDTH, ROWS), BF16),
            pltpu.VMEM((2, 64, 16, 128), BF16),
            pltpu.VMEM((2, 16, 128), BF16),
            pltpu.VMEM((2, WIDTH, ROWS), BF16),
            pltpu.SemaphoreType.REGULAR((6,)),
            dma((8,)),
            dma((3,)), dma((3,)), dma((3,)), dma((3,)), dma((3,)), dma((3,)),
            dma((2,)), dma((2,)), dma((2,)), dma((2,)),
            dma((2, 2)), dma((2, 2)), dma((2,)), dma((2,)), dma((2,)), dma((2,)),
        ],
        compiler_params=pltpu.CompilerParams(
            collective_id=0, has_side_effects=True, vmem_limit_bytes=47 * 1024 * 1024
        ),
    )(*[pltpu.with_memory_space_constraint(a, pltpu.HBM) for a in arrays])
    code_array = jax.ShapeDtypeStruct(code_shape, F32)
    return pl.pallas_call(
        write_out,
        name="write_out",
        out_shape=(jax.ShapeDtypeStruct(rows_shape, BF16), code_array, code_array, code_array),
        in_specs=[vmem_spec] * 4,
        out_specs=[any_spec] * 4,
        scratch_shapes=[dma((4,))],
        compiler_params=pltpu.CompilerParams(vmem_limit_bytes=8 * 1024 * 1024),
    )(*[pltpu.with_memory_space_constraint(p, pltpu.VMEM) for p in parts])


def solution(mesh):
    rows, codes = P(None, "dp", None), P(("dp", "code"), None)
    def run(*arrays):
        with jax.sharding.use_abstract_mesh(mesh.abstract_mesh):
            return body(*arrays)

    return jax.shard_map(
        run,
        mesh=mesh,
        in_specs=(rows, rows, P(None, "dp"), codes, codes, codes),
        out_specs=(rows, codes, codes, codes),
        check_vma=False,
    )
```
